256 devices in a mesh: fsdp: 16 (over z_hi, x, core), expert: 16 (over z_lo, y).
Axes of the slice: x: 4, y: 4, z: 8 (z_hi: 2, z_lo: 4; z = z_hi * 4 + z_lo), core: 2. Of those that a mesh axis runs over, the one named last changes fastest.
Arguments:
- out_grad: bfloat16 [32768, 4096], P(('fsdp', 'expert')), may hold values from -1.5 to 1.5
- router_probs: bfloat16 [32768, 8], P(('fsdp', 'expert')), may hold values from 0.049804688 to 0.59765625
- expert_ids: int32 [32768, 8], P(('fsdp', 'expert')), may hold values from 0 to 127, as said below
- saved_hidden: bfloat16 [16, 16, 256, 2048], P('fsdp', 'expert'), may hold values from -6 to 6
- w_down: bfloat16 [16, 4096, 1024], P('expert', 'fsdp'), may hold values from -0.1875 to 0.1875
Outputs:
- dprobs: float32 [32768, 8], P(('fsdp', 'expert'))
- grad_pre: bfloat16 [16, 16, 256, 2048], P('fsdp', 'expert')
- grad_down: float32 [16, 4096, 1024], P('expert', 'fsdp')
The draws below stay inside these ranges and needn't reach their ends.
Inputs may be any that keep to these rules, and one draw needn't show every extreme that they name: `expert_ids`: each row names 8 different experts. In every aligned block of 128 rows (the tokens of one device) some expert below 16 is named by 16 rows or more.
All inputs are finite; a program needn't handle non-finite values.
Results may differ from the reference program's by a relative error of at most 0.01.
Values may be sent and summed in bfloat16 or wider, within the bound.
A program may use at most 128 MiB of HBM per device.

```python
import math
import jax
import jax.numpy as jnp
from jax import lax

D = 4096
EXPERT_TOTAL = 128
TOP = 8
HW = 1024
TOK_DEV = 128
CAP = 16
EXPERTS = 16
SLOTS = 256
GROUPS = 16
TOKENS = 32768
N_FSDP = 16
N_EXPERT = 16


def draw_expert_ids(key, part):
    block_count = TOKENS // TOK_DEV
    keys = jax.random.split(key, 4)
    random_jitter = jax.random.randint(keys[0], (TOKENS, EXPERT_TOTAL), 0, 2 ** 18, dtype=jnp.int32)
    favored_experts = jax.random.randint(keys[1], (EXPERT_TOTAL,), 0, 5, dtype=jnp.int32) * 2 ** 17
    busiest_expert = jax.random.randint(keys[2], (), 0, EXPERTS, dtype=jnp.int32)

    def block_marks(block_key):
        return jax.random.permutation(block_key, TOK_DEV) < CAP
    marker_flags = jax.vmap(block_marks)(jax.random.split(keys[3], block_count)).reshape(TOKENS)
    column_list = jnp.arange(EXPERT_TOTAL, dtype=jnp.int32)
    extra_boost = jnp.where(marker_flags[:, None] & (column_list[None, :] == busiest_expert), 2 ** 21, 0).astype(jnp.int32)
    router_logits = (random_jitter + favored_experts[None, :] + extra_boost) * EXPERT_TOTAL + column_list[None, :]
    values, chosen = lax.top_k(router_logits, TOP)
    return chosen.astype(jnp.int32)


def level_of(stream_key, shape, cuts, least, top_value):
    factor_of = 1.0
    for dim, blocks in cuts:
        draws = jax.random.uniform(jax.random.fold_in(jax.random.fold_in(stream_key, 6), dim), (blocks,), jnp.float32, least / len(cuts), top_value / len(cuts))
        factor_of = factor_of * jnp.repeat(jnp.exp(draws), shape[dim] // blocks).reshape((-1,) + (1,) * (len(shape) - 1 - dim))
    return factor_of


def bell_draw(own_key, extent, deviation, most, cuts=(), kind=jnp.bfloat16):
    gain = level_of(own_key, extent, cuts, -0.22, 0.18) if cuts else 1.0
    result = jax.random.normal(own_key, extent, jnp.float32) * deviation * gain
    return jnp.minimum(jnp.maximum(result, -most), most).astype(kind)


def setup_inputs(seed: int = 0) -> dict:
    key_of = jax.random.split(jax.random.key(seed), 6)
    out_grad = bell_draw(key_of[0], (TOKENS, D), 0.25, 1.5, ((0, 256),))
    router_probs = jnp.clip(jnp.exp(math.log(0.59765625) - 2.4849066 * jax.random.uniform(key_of[1], (TOKENS, TOP), jnp.float32) ** level_of(key_of[1], (TOKENS, TOP), ((0, 256),), -0.2, 0.2)), 0.049804688, 0.59765625).astype(jnp.bfloat16)
    expert_ids = draw_expert_ids(jax.random.fold_in(key_of[5], 71), 0)
    saved_hidden = bell_draw(key_of[3], (GROUPS, EXPERTS, SLOTS, 2 * HW), 1.0, 6.0, ((0, 16), (1, 16)))
    w_down = bell_draw(key_of[4], (EXPERTS, D, HW), HW ** -0.5, 0.1875, ((0, 16), (1, 16)))
    return {"out_grad": out_grad, "router_probs": router_probs, "expert_ids": expert_ids, "saved_hidden": saved_hidden, "w_down": w_down}


def route_block(block_ids, experts, capacity):
    flat_ids = block_ids.reshape(-1)
    onehot = (flat_ids[:, None] == jnp.arange(experts, dtype=jnp.int32)[None, :]).astype(jnp.int32)
    before = jnp.sum((jnp.cumsum(onehot, axis=0) - onehot) * onehot, axis=1)
    is_kept = (flat_ids < experts) & (before < capacity)
    slot_of = jnp.where(is_kept, flat_ids * capacity + before, experts * capacity).astype(jnp.int32)
    source = jnp.arange(flat_ids.shape[0], dtype=jnp.int32)
    row_of = jnp.zeros((experts * capacity,), jnp.int32).at[slot_of].set(source, mode="drop")
    filled = jnp.zeros((experts * capacity,), jnp.int32).at[slot_of].set(jnp.ones_like(source), mode="drop")
    return slot_of, row_of, filled


def reference(out_grad, router_probs, expert_ids, saved_hidden, w_down):
    block_count = N_FSDP * N_EXPERT
    ids_blocks = expert_ids.reshape(block_count, TOK_DEV, TOP)
    slot_of, row_of, filled = jax.vmap(lambda blocked: route_block(blocked, EXPERTS, CAP))(ids_blocks)
    grad_blocks = out_grad.reshape(block_count, TOK_DEV, D)
    prob_blocks = router_probs.reshape(block_count, TOK_DEV * TOP)

    def place(grads, probs_row, rows_of, fills):
        live = fills.astype(jnp.bfloat16)
        return grads[rows_of // TOP] * live[:, None], probs_row[rows_of] * live

    routed, weight = jax.vmap(place)(grad_blocks, prob_blocks, row_of, filled)
    routed = routed.reshape(N_FSDP, N_EXPERT, EXPERTS, CAP, D).transpose(2, 0, 1, 3, 4).reshape(EXPERTS, N_FSDP, SLOTS, D)
    weight = weight.reshape(N_FSDP, N_EXPERT, EXPERTS, CAP).transpose(2, 0, 1, 3).reshape(EXPERTS, N_FSDP * SLOTS)
    hidden_by_expert = saved_hidden.transpose(1, 0, 2, 3)

    def per_expert(inputs):
        routed_e, weight_e, hidden_e, matrix = inputs
        rows_e = routed_e.reshape(N_FSDP * SLOTS, D)
        gate_pre = hidden_e[..., :HW].reshape(N_FSDP * SLOTS, HW).astype(jnp.float32)
        up_pre = hidden_e[..., HW:].reshape(N_FSDP * SLOTS, HW).astype(jnp.float32)
        sigma = jax.nn.sigmoid(gate_pre)
        activation = (gate_pre * sigma * up_pre).astype(jnp.bfloat16)
        probs_col = weight_e.astype(jnp.float32)[:, None]
        scaled = (probs_col * rows_e.astype(jnp.float32)).astype(jnp.bfloat16)
        back_grad = jnp.dot(rows_e, matrix, preferred_element_type=jnp.float32)
        slot_grad = jnp.sum(activation.astype(jnp.float32) * back_grad, axis=1)
        grad_hidden = probs_col * back_grad
        grad_gate = grad_hidden * up_pre * sigma * (1.0 + gate_pre * (1.0 - sigma))
        grad_up = grad_hidden * gate_pre * sigma
        grad_part = jnp.concatenate([grad_gate, grad_up], axis=1).astype(jnp.bfloat16).reshape(N_FSDP, SLOTS, 2 * HW)
        grad_matrix = jnp.dot(scaled.T, activation, preferred_element_type=jnp.float32)
        return grad_part, slot_grad.reshape(N_FSDP, SLOTS), grad_matrix

    grad_pre, slot_grad, grad_down = lax.map(per_expert, (routed, weight, hidden_by_expert, w_down))
    grad_pre = grad_pre.transpose(1, 0, 2, 3)
    back_blocks = slot_grad.reshape(EXPERTS, N_FSDP, N_EXPERT, CAP).transpose(1, 2, 0, 3).reshape(block_count, EXPERTS * CAP)

    def unplace(values, slots):
        safe = jnp.minimum(slots, EXPERTS * CAP - 1)
        return jnp.where(slots < EXPERTS * CAP, values[safe], jnp.zeros((), values.dtype))

    dprobs = jax.vmap(unplace)(back_blocks, slot_of).reshape(TOKENS, TOP)
    return dprobs, grad_pre, grad_down
```

```python
import jax
import jax.numpy as jnp
from jax import lax
from jax.experimental import pallas as pl
from jax.experimental.pallas import tpu as pltpu
from jax.sharding import PartitionSpec as P

F32 = jnp.float32
BF16 = jnp.bfloat16
MESH = pl.DeviceIdType.MESH
CAP = 16
NX = 4
STAGES = ((0, 0, 4), (1, 2, 1), (1, 1, 1), (1, 3, 1), (1, 0, 1))
WSTAGE = len(STAGES)


def kernel(
    ids_ref, probs_ref, og_hbm, hid_hbm, w_hbm,
    dp_out, gp_out, gd_out,
    meta, ogb, gbuf, wsend, wbuf, sendbuf, routed, hidv, act, bvec, wq, sct, pown,
    csend, crecv, zsend, zrecv, bp, bsend, brecv, sgb, ret,
    hid_sem, meta_s, meta_r, og_s, og_r, w_s, w_r, act_s, act_r, a_s, a_r,
    c_s, c_r, z_s, z_r, b_s, b_r, ret_s, ret_r,
):
    ne = 16
    f = lax.axis_index("fsdp")
    e = lax.axis_index("expert")
    zh, x, c = f // 8, (f // 2) % 4, f % 2

    def at_x(d):
        return (zh * 8 + ((x + d) % 4) * 2 + c, e)

    z_peer = ((1 - zh) * 8 + x * 2 + c, e)
    sibling = (zh * 8 + x * 2 + 1 - c, e)

    def remote(src, dst, ss, rs, dev):
        return pltpu.make_async_remote_copy(
            src_ref=src, dst_ref=dst, send_sem=ss, recv_sem=rs, device_id=dev, device_id_type=MESH
        )

    def drain(ref, sem):
        pltpu.make_async_copy(ref, ref, sem).wait()

    own_w = pltpu.make_async_copy(w_hbm, wq.at[:, pl.ds(0, 128), :], w_r.at[0])
    own_hid = pltpu.make_async_copy(hid_hbm, hidv, hid_sem)

    def og_columns(xt, b):
        dz, dc = b % 2, b // 2
        col = ((zh + dz) % 2) * 2048 + xt * 512 + ((c + dc) % 2) * 256
        return og_hbm.at[:, pl.ds(pl.multiple_of(col, 256), 256)]

    for b in range(4):
        pltpu.make_async_copy(og_columns(x, b), ogb.at[0, b], og_r.at[0]).start()
    own_hid.start()
    own_w.start()
    meta[0, 0:8, :] = ids_ref[...].astype(F32)
    meta[0, 8:16, :] = probs_ref[...].astype(F32)

    barrier = pltpu.get_barrier_semaphore()
    for d in (1, 2, 3):
        pl.semaphore_signal(barrier, inc=1, device_id=at_x(d), device_id_type=MESH)
    pl.semaphore_signal(barrier, inc=1, device_id=z_peer, device_id_type=MESH)
    pl.semaphore_signal(barrier, inc=1, device_id=sibling, device_id_type=MESH)

    def greet(k, carry):
        pl.semaphore_signal(barrier, inc=1, device_id=(f, (e + k) % ne), device_id_type=MESH)
        return carry

    lax.fori_loop(1, ne, greet, 0)
    pl.semaphore_wait(barrier, 5 + ne - 1)

    for d in (2, 1, 3):
        remote(meta.at[0], meta.at[4 - d], meta_s.at[d], meta_r.at[4 - d], at_x(d)).start()
    for d in (2, 1, 3):
        for b in range(4):
            remote(
                og_columns((x + d) % 4, b), ogb.at[4 - d, b], og_s.at[d], og_r.at[4 - d], at_x(d)
            ).start()
    remote(w_hbm, wq.at[:, pl.ds(128, 128), :], w_s.at[0], w_r.at[1], z_peer).start()
    remote(w_hbm, wq.at[:, pl.ds(256, 128), :], w_s.at[1], w_r.at[2], sibling).start()

    tri_r = lax.broadcasted_iota(jnp.int32, (128, 128), 0)
    tri_c = lax.broadcasted_iota(jnp.int32, (128, 128), 1)
    upper = jnp.where(tri_r < tri_c, 1.0, 0.0).astype(BF16)
    e_iota = lax.broadcasted_iota(jnp.int32, (ne, 128), 0).astype(F32)
    r_iota = lax.broadcasted_iota(jnp.int32, (ne, CAP, 128), 1).astype(F32)
    lane = lax.broadcasted_iota(jnp.int32, (ne * CAP, 128), 1)
    wacc = jnp.zeros((ne * CAP, 128), F32)
    for d in (0, 1, 3, 2):
        if d:
            drain(meta.at[d], meta_r.at[d])
        ids8 = meta[d, 0:8, :]
        pr8 = meta[d, 8:16, :]
        named = jnp.zeros((ne, 128), F32)
        prob = jnp.zeros((ne, 128), F32)
        for k in range(8):
            hit = ids8[k : k + 1, :] == e_iota
            named = named + jnp.where(hit, 1.0, 0.0)
            prob = prob + jnp.where(hit, pr8[k : k + 1, :], 0.0)
        rank = jnp.dot(named.astype(BF16), upper, preferred_element_type=F32)
        rank = jnp.where(named > 0.0, rank, -1.0)
        pick = jnp.where(rank[:, None, :] == r_iota, 1.0, 0.0)
        wcol = jnp.sum((pick * prob[:, None, :]).reshape(ne * CAP, 128), axis=1, keepdims=True)
        wacc = jnp.where(lane == d, wcol, wacc)
        gbuf[d] = pick.reshape(ne * CAP, 128).astype(BF16)
    wsend[...] = wacc.astype(BF16)

    for d in (0, 1, 3, 2):
        drain(ogb.at[d], og_r.at[d])
        g = gbuf[d]
        for b in range(4):
            rows = jnp.dot(g, ogb[d, b], preferred_element_type=F32).astype(BF16)
            sendbuf[0, d, :, b * 128 : b * 128 + 128] = rows[:, :128]
            sendbuf[1, d, :, b * 128 : b * 128 + 128] = rows[:, 128:]

    def my_rows(ref, h, d0, dn, who):
        return ref.at[h, pl.ds(d0, dn), pl.ds(pl.multiple_of(who * CAP, CAP), CAP), :]

    def wrows(ref, who):
        return ref.at[pl.ds(pl.multiple_of(who * CAP, CAP), CAP), :]

    def exchange(first, count):
        for i in range(first, first + count):
            h, d0, dn = STAGES[i]
            pltpu.make_async_copy(
                my_rows(sendbuf, h, d0, dn, e), my_rows(routed, h, d0, dn, e), a_r.at[i]
            ).start()

            def send(k, carry):
                to = (e + k) % ne
                remote(
                    my_rows(sendbuf, h, d0, dn, to),
                    my_rows(routed, h, d0, dn, e),
                    a_s.at[i],
                    a_r.at[i],
                    (f, to),
                ).start()
                return carry

            lax.fori_loop(1, ne, send, 0)

    def arrived(i):
        h, d0, dn = STAGES[i]
        drain(routed.at[h, pl.ds(d0, dn)], a_r.at[i])

    pltpu.make_async_copy(wrows(wsend, e), wrows(wbuf, e), a_r.at[WSTAGE]).start()

    def send_weight(k, carry):
        to = (e + k) % ne
        remote(
            wrows(wsend, to), wrows(wbuf, e), a_s.at[WSTAGE], a_r.at[WSTAGE], (f, to)
        ).start()
        return carry

    lax.fori_loop(1, ne, send_weight, 0)
    exchange(0, len(STAGES))

    own_hid.wait()

    def activate(i, carry):
        rows = pl.ds(pl.multiple_of(i * 16, 16), 16)
        gate = hidv[rows, 0:1024].astype(F32)
        up = hidv[rows, 1024:2048].astype(F32)
        sigma = jax.nn.sigmoid(gate)
        silu = gate * sigma
        act[rows, :] = (silu * up).astype(BF16)
        bvec[rows, 0:1024] = up * sigma * (1.0 + gate * (1.0 - sigma))
        bvec[rows, 1024:2048] = silu
        return carry

    lax.fori_loop(0, 16, activate, 0)
    for d in (2, 1, 3):
        remote(
            act.at[pl.ds(0, 256)],
            act.at[pl.ds((4 - d) * 256, 256)],
            act_s.at[d],
            act_r.at[4 - d],
            at_x(d),
        ).start()

    drain(wq.at[:, pl.ds(128, 128), :], w_r.at[1])
    remote(
        wq.at[:, pl.ds(128, 128), :], wq.at[:, pl.ds(384, 128), :], w_s.at[2], w_r.at[3], sibling
    ).start()
    drain(wbuf, a_r.at[WSTAGE])
    own_w.wait()
    drain(wq.at[:, pl.ds(256, 128), :], w_r.at[2])
    drain(wq.at[:, pl.ds(384, 128), :], w_r.at[3])

    def scale(h, d):
        wcol = wbuf[:, d : d + 1].astype(F32)
        for b in range(4):
            part = routed[h, d, :, b * 128 : b * 128 + 128].astype(F32) * wcol
            sct[h, b * 128 : b * 128 + 128, d * 256 : d * 256 + 256] = part.T.astype(BF16)

    def back_part(h, d, n):
        cols = pl.ds(pl.multiple_of(n * 256, 256), 256)
        return jnp.dot(routed[h, d], wq[h, :, cols], preferred_element_type=F32), cols

    def grad_down_part(h):
        def sib(n, carry):
            cols = pl.ds(pl.multiple_of(n * 256, 256), 256)
            csend[h, :, cols] = jnp.dot(
                sct[h, 256:512, :], act[:, cols], preferred_element_type=F32
            ).astype(BF16)
            return carry

        lax.fori_loop(0, 4, sib, 0)
        remote(csend.at[h], crecv.at[h], c_s.at[h], c_r.at[h], sibling).start()

        def own(n, carry):
            cols = pl.ds(pl.multiple_of(n * 256, 256), 256)
            pown[h, :, cols] = jnp.dot(sct[h, 0:256, :], act[:, cols], preferred_element_type=F32)
            return carry

        lax.fori_loop(0, 4, own, 0)

    def over_z(h):
        drain(crecv.at[h], c_r.at[h])

        def add(n, carry):
            rows = pl.ds(pl.multiple_of(n * 16, 16), 16)
            rows2 = pl.ds(pl.multiple_of(128 + n * 16, 16), 16)
            zsend[h, rows, :] = (pown[h, rows2, :] + crecv[h, rows2, :].astype(F32)).astype(BF16)
            return carry

        lax.fori_loop(0, 8, add, 0)
        remote(zsend.at[h], zrecv.at[h], z_s.at[h], z_r.at[h], z_peer).start()

    for d in (1, 2, 3):
        drain(act.at[pl.ds(d * 256, 256)], act_r.at[d])
    arrived(0)
    for d in range(4):
        scale(0, d)
    grad_down_part(0)
    for d in range(4):

        def back0(n, carry, d=d):
            part, cols = back_part(0, d, n)
            bp[d, :, cols] = part
            return carry

        lax.fori_loop(0, 4, back0, 0)
        if d == 0:
            over_z(0)

    for i in range(1, len(STAGES)):
        d = STAGES[i][1]
        arrived(i)
        scale(1, d)
        if d:

            def back1(n, carry, d=d):
                part, cols = back_part(1, d, n)
                bsend[d - 1, :, cols] = (bp[d, :, cols] + part).astype(BF16)
                return carry

            lax.fori_loop(0, 4, back1, 0)
            remote(
                bsend.at[d - 1], brecv.at[3 - d], b_s.at[d - 1], b_r.at[3 - d], at_x(d)
            ).start()
    grad_down_part(1)

    def back_own(n, carry):
        part, cols = back_part(1, 0, n)
        bp[0, :, cols] = bp[0, :, cols] + part
        return carry

    lax.fori_loop(0, 4, back_own, 0)
    over_z(1)

    for d in range(3):
        drain(brecv.at[d], b_r.at[d])

    def finish(i, carry):
        rows = pl.ds(pl.multiple_of(i * 16, 16), 16)
        back = bp[0, rows, :] + brecv[0, rows, :].astype(F32)
        back = back + brecv[1, rows, :].astype(F32) + brecv[2, rows, :].astype(F32)
        slot_grad = jnp.sum(act[rows, :].astype(F32) * back, axis=1, keepdims=True)
        sgb[rows, :] = jnp.broadcast_to(slot_grad, (16, 128))
        hidden = wbuf[rows, 0:1].astype(F32) * back
        gp_out[rows, 0:1024] = (hidden * bvec[rows, 0:1024]).astype(BF16)
        gp_out[rows, 1024:2048] = (hidden * bvec[rows, 1024:2048]).astype(BF16)
        return carry

    lax.fori_loop(0, 16, finish, 0)

    pltpu.make_async_copy(wrows(sgb, e), wrows(ret, e), ret_r).start()

    def send_back(k, carry):
        to = (e + k) % ne
        remote(wrows(sgb, to), wrows(ret, e), ret_s, ret_r, (f, to)).start()
        return carry

    lax.fori_loop(1, ne, send_back, 0)

    for h in range(2):
        drain(zrecv.at[h], z_r.at[h])

        def total(n, carry):
            rows = pl.ds(pl.multiple_of(n * 16, 16), 16)
            mine = pown[h, rows, :] + crecv[h, rows, :].astype(F32)
            gd_out[pl.ds(pl.multiple_of(h * 128 + n * 16, 16), 16), :] = mine + zrecv[
                h, rows, :
            ].astype(F32)
            return carry

        lax.fori_loop(0, 8, total, 0)

    drain(ret, ret_r)
    per_slot = (gbuf[0].astype(F32) * ret[...]).reshape(ne, CAP, 128)
    per_expert = jnp.sum(per_slot, axis=1)
    ids8 = meta[0, 0:8, :]
    dp = jnp.zeros((8, 128), F32)
    for k in range(ne):
        dp = dp + jnp.where(ids8 == float(k), per_expert[k : k + 1, :], 0.0)
    dp_out[...] = dp

    for d in (1, 2, 3):
        drain(meta.at[0], meta_s.at[d])
        drain(ogb.at[0], og_s.at[d])
        drain(act.at[pl.ds(0, 256)], act_s.at[d])
        drain(bsend.at[0], b_s.at[d - 1])
    for i in range(3):
        drain(wq.at[:, pl.ds(0, 128), :], w_s.at[i])
    for h in range(2):
        drain(csend.at[h], c_s.at[h])
        drain(zsend.at[h], z_s.at[h])
    for i, (h, d0, dn) in enumerate(STAGES):
        drain(sendbuf.at[h, pl.ds(d0, dn), pl.ds(0, (ne - 1) * CAP), :], a_s.at[i])
    drain(wsend.at[pl.ds(0, (ne - 1) * CAP)], a_s.at[WSTAGE])
    drain(sgb.at[pl.ds(0, (ne - 1) * CAP)], ret_s)


def per_device(out_grad, router_probs, expert_ids, saved_hidden, w_down):
    dma = pltpu.SemaphoreType.DMA
    vmem = pl.BlockSpec(memory_space=pltpu.VMEM)
    hbm = pl.BlockSpec(memory_space=pl.ANY)
    stages = len(STAGES) + 1
    dp, gp, gd = pl.pallas_call(
        kernel,
        out_shape=(
            jax.ShapeDtypeStruct((8, 128), F32),
            jax.ShapeDtypeStruct((256, 2048), BF16),
            jax.ShapeDtypeStruct((256, 1024), F32),
        ),
        in_specs=[vmem, vmem, hbm, hbm, hbm],
        out_specs=(vmem, vmem, vmem),
        scratch_shapes=[
            pltpu.VMEM((4, 16, 128), F32),
            pltpu.VMEM((4, 4, 128, 256), BF16),
            pltpu.VMEM((4, 256, 128), BF16),
            pltpu.VMEM((256, 128), BF16),
            pltpu.VMEM((256, 128), BF16),
            pltpu.VMEM((2, 4, 256, 512), BF16),
            pltpu.VMEM((2, 4, 256, 512), BF16),
            pltpu.VMEM((256, 2048), BF16),
            pltpu.VMEM((1024, 1024), BF16),
            pltpu.VMEM((256, 2048), F32),
            pltpu.VMEM((2, 512, 1024), BF16),
            pltpu.VMEM((2, 512, 1024), BF16),
            pltpu.VMEM((2, 256, 1024), F32),
            pltpu.VMEM((2, 256, 1024), BF16),
            pltpu.VMEM((2, 256, 1024), BF16),
            pltpu.VMEM((2, 128, 1024), BF16),
            pltpu.VMEM((2, 128, 1024), BF16),
            pltpu.VMEM((4, 256, 1024), F32),
            pltpu.VMEM((3, 256, 1024), BF16),
            pltpu.VMEM((3, 256, 1024), BF16),
            pltpu.VMEM((256, 128), F32),
            pltpu.VMEM((256, 128), F32),
            dma,
            dma((4,)), dma((4,)),
            dma((4,)), dma((4,)),
            dma((3,)), dma((4,)),
            dma((4,)), dma((4,)),
            dma((stages,)), dma((stages,)),
            dma((2,)), dma((2,)),
            dma((2,)), dma((2,)),
            dma((3,)), dma((3,)),
            dma, dma,
        ],
        compiler_params=pltpu.CompilerParams(
            collective_id=0, has_side_effects=True, vmem_limit_bytes=56 * 2**20
        ),
    )(
        expert_ids.T,
        router_probs.T,
        out_grad,
        saved_hidden.reshape(256, 2048),
        w_down.reshape(2, 128, 1024),
    )
    return dp.T, gp.reshape(1, 1, 256, 2048), gd.reshape(1, 256, 1024)


def solution(mesh):
    placed = (
        P(("fsdp", "expert"), None),
        P(("fsdp", "expert"), None),
        P(("fsdp", "expert"), None),
        P("fsdp", "expert", None, None),
        P("expert", "fsdp", None),
    )
    return jax.shard_map(
        per_device,
        mesh=mesh,
        in_specs=placed,
        out_specs=(
            P(("fsdp", "expert"), None),
            P("fsdp", "expert", None, None),
            P("expert", "fsdp", None),
        ),
        check_vma=False,
    )
```

```python
import jax
import jax.numpy as jnp
from jax import lax
from jax.experimental import pallas as pl
from jax.experimental.pallas import tpu as pltpu
from jax.sharding import PartitionSpec as P

F32 = jnp.float32
BF16 = jnp.bfloat16
MESH = pl.DeviceIdType.MESH
CAP = 16
NX = 4
STAGES = ((0, 0, 4), (1, 2, 1), (1, 1, 1), (1, 3, 1), (1, 0, 1))
WSTAGE = len(STAGES)
ZAT = (4, 4)
ZPARTS = len(ZAT)
ZROWS = 256 // ZPARTS


def kernel(
    ids_hbm, probs_hbm, og_hbm, hid_hbm, w_hbm,
    dp_out, gp_out, gd_out,
    meta, ogb, gbuf, wsend, wbuf, sendbuf, routed, hidv, act, bvec, wq, sct, pown,
    csend, crecv, zsend, zrecv, bp, bsend, brecv, sgb, ret,
    ids_ref, probs_ref, in_sem, hid_sem, meta_s, meta_r, og_s, og_r, w_s, w_r, act_s, act_r, a_s, a_r,
    c_s, c_r, z_s, z_r, b_s, b_r, ret_s, ret_r,
):
    ne = 16
    f = lax.axis_index("fsdp")
    e = lax.axis_index("expert")
    zh, x, c = f // 8, (f // 2) % 4, f % 2

    def at_x(d):
        return (zh * 8 + ((x + d) % 4) * 2 + c, e)

    z_peer = ((1 - zh) * 8 + x * 2 + c, e)
    sibling = (zh * 8 + x * 2 + 1 - c, e)

    def remote(src, dst, ss, rs, dev):
        return pltpu.make_async_remote_copy(
            src_ref=src, dst_ref=dst, send_sem=ss, recv_sem=rs, device_id=dev, device_id_type=MESH
        )

    def drain(ref, sem):
        pltpu.make_async_copy(ref, ref, sem).wait()

    own_w = pltpu.make_async_copy(w_hbm, wq.at[1, pl.ds(0, 256), :], w_r.at[0])
    own_hid = pltpu.make_async_copy(hid_hbm, hidv, hid_sem)

    def og_columns(xt, h):
        col = ((zh + 1 - h) % 2) * 2048 + xt * 512
        return og_hbm.at[:, pl.ds(pl.multiple_of(col, 512), 512)]

    barrier = pltpu.get_barrier_semaphore()
    for d in (1, 2, 3):
        pl.semaphore_signal(barrier, inc=1, device_id=at_x(d), device_id_type=MESH)
    pl.semaphore_signal(barrier, inc=1, device_id=z_peer, device_id_type=MESH)
    pl.semaphore_signal(barrier, inc=1, device_id=sibling, device_id_type=MESH)

    def greet(k, carry):
        pl.semaphore_signal(barrier, inc=1, device_id=(f, (e + k) % ne), device_id_type=MESH)
        return carry

    lax.fori_loop(1, ne, greet, 0)
    for h in range(2):
        pltpu.make_async_copy(og_columns(x, h), ogb.at[0, h], og_r.at[h, 0]).start()
    own_hid.start()
    own_w.start()
    own_ids = pltpu.make_async_copy(ids_hbm, ids_ref, in_sem.at[0])
    own_probs = pltpu.make_async_copy(probs_hbm, probs_ref, in_sem.at[1])
    own_ids.start()
    own_probs.start()
    own_ids.wait()
    own_probs.wait()
    meta[0, 0:8, :] = ids_ref[...].astype(F32)
    meta[0, 8:16, :] = probs_ref[...].astype(F32)
    pl.semaphore_wait(barrier, 5 + ne - 1)

    for d in (2, 1, 3):
        remote(meta.at[0], meta.at[4 - d], meta_s.at[d], meta_r.at[4 - d], at_x(d)).start()
    for h in range(2):
        for d in (2, 1, 3):
            remote(
                og_columns((x + d) % 4, h),
                ogb.at[4 - d, h],
                og_s.at[h, d],
                og_r.at[h, 4 - d],
                at_x(d),
            ).start()
        if h == 0:
            remote(w_hbm, wq.at[0, pl.ds(0, 256), :], w_s.at[0], w_r.at[1], z_peer).start()
            remote(w_hbm, wq.at[1, pl.ds(256, 256), :], w_s.at[1], w_r.at[2], sibling).start()

    tri_r = lax.broadcasted_iota(jnp.int32, (128, 128), 0)
    tri_c = lax.broadcasted_iota(jnp.int32, (128, 128), 1)
    upper = jnp.where(tri_r < tri_c, 1.0, 0.0).astype(BF16)
    e_iota = lax.broadcasted_iota(jnp.int32, (ne, 128), 0).astype(F32)
    r_iota = lax.broadcasted_iota(jnp.int32, (ne, CAP, 128), 1).astype(F32)
    lane = lax.broadcasted_iota(jnp.int32, (ne * CAP, 128), 1)
    wacc = jnp.zeros((ne * CAP, 128), F32)
    for d in (0, 1, 3, 2):
        if d:
            drain(meta.at[d], meta_r.at[d])
        ids8 = meta[d, 0:8, :]
        pr8 = meta[d, 8:16, :]
        named = jnp.zeros((ne, 128), F32)
        prob = jnp.zeros((ne, 128), F32)
        for k in range(8):
            hit = ids8[k : k + 1, :] == e_iota
            named = named + jnp.where(hit, 1.0, 0.0)
            prob = prob + jnp.where(hit, pr8[k : k + 1, :], 0.0)
        rank = jnp.dot(named.astype(BF16), upper, preferred_element_type=F32)
        rank = jnp.where(named > 0.0, rank, -1.0)
        pick = jnp.where(rank[:, None, :] == r_iota, 1.0, 0.0)
        wcol = jnp.sum((pick * prob[:, None, :]).reshape(ne * CAP, 128), axis=1, keepdims=True)
        wacc = jnp.where(lane == d, wcol, wacc)
        gbuf[d] = pick.reshape(ne * CAP, 128).astype(BF16)
    wsend[...] = wacc.astype(BF16)

    def expand(h):
        for d in (0, 1, 3, 2):
            drain(ogb.at[d, h], og_r.at[h, d])
            for dc in range(2):
                columns = pl.ds(pl.multiple_of(((c + dc) % 2) * 256, 256), 256)
                sendbuf[h, d, :, dc * 256 : dc * 256 + 256] = jnp.dot(
                    gbuf[d], ogb[d, h, :, columns], preferred_element_type=F32
                ).astype(BF16)

    def my_rows(ref, h, d0, dn, who):
        return ref.at[h, pl.ds(d0, dn), pl.ds(pl.multiple_of(who * CAP, CAP), CAP), :]

    def wrows(ref, who):
        return ref.at[pl.ds(pl.multiple_of(who * CAP, CAP), CAP), :]

    def exchange(first, count):
        for i in range(first, first + count):
            h, d0, dn = STAGES[i]
            pltpu.make_async_copy(
                my_rows(sendbuf, h, d0, dn, e), my_rows(routed, h, d0, dn, e), a_r.at[i]
            ).start()

            def send(k, carry):
                to = (e + k) % ne
                remote(
                    my_rows(sendbuf, h, d0, dn, to),
                    my_rows(routed, h, d0, dn, e),
                    a_s.at[i],
                    a_r.at[i],
                    (f, to),
                ).start()
                return carry

            lax.fori_loop(1, ne, send, 0)

    def arrived(i):
        h, d0, dn = STAGES[i]
        drain(routed.at[h, pl.ds(d0, dn)], a_r.at[i])

    pltpu.make_async_copy(wrows(wsend, e), wrows(wbuf, e), a_r.at[WSTAGE]).start()

    def send_weight(k, carry):
        to = (e + k) % ne
        remote(
            wrows(wsend, to), wrows(wbuf, e), a_s.at[WSTAGE], a_r.at[WSTAGE], (f, to)
        ).start()
        return carry

    lax.fori_loop(1, ne, send_weight, 0)
    expand(0)
    exchange(0, 1)
    expand(1)
    exchange(1, 1)

    own_hid.wait()

    def activate(i, carry):
        rows = pl.ds(pl.multiple_of(i * 16, 16), 16)
        gate = hidv[rows, 0:1024].astype(F32)
        up = hidv[rows, 1024:2048].astype(F32)
        sigma = jax.nn.sigmoid(gate)
        silu = gate * sigma
        act[rows, :] = (silu * up).astype(BF16)
        bvec[rows, 0:1024] = up * sigma * (1.0 + gate * (1.0 - sigma))
        bvec[rows, 1024:2048] = silu
        return carry

    lax.fori_loop(0, 16, activate, 0)
    for d in (2, 1, 3):
        remote(
            act.at[pl.ds(0, 256)],
            act.at[pl.ds((4 - d) * 256, 256)],
            act_s.at[d],
            act_r.at[4 - d],
            at_x(d),
        ).start()

    drain(wq.at[0, pl.ds(0, 256), :], w_r.at[1])
    remote(
        wq.at[0, pl.ds(0, 256), :], wq.at[0, pl.ds(256, 256), :], w_s.at[2], w_r.at[3], sibling
    ).start()
    drain(wbuf, a_r.at[WSTAGE])
    own_w.wait()
    drain(wq.at[1, pl.ds(256, 256), :], w_r.at[2])
    drain(wq.at[0, pl.ds(256, 256), :], w_r.at[3])

    def scale(h, d):
        wcol = wbuf[:, d : d + 1].astype(F32)
        for b in range(4):
            part = routed[h, d, :, b * 128 : b * 128 + 128].astype(F32) * wcol
            sct[h, b * 128 : b * 128 + 128, d * 256 : d * 256 + 256] = part.T.astype(BF16)

    def back_part(h, d, n):
        cols = pl.ds(pl.multiple_of(n * 256, 256), 256)
        return jnp.dot(routed[h, d], wq[h, :, cols], preferred_element_type=F32), cols

    def grad_down_part(h):
        def sib(n, carry):
            cols = pl.ds(pl.multiple_of(n * 256, 256), 256)
            csend[h, :, cols] = jnp.dot(
                sct[h, 256:512, :], act[:, cols], preferred_element_type=F32
            ).astype(BF16)
            return carry

        lax.fori_loop(0, 4, sib, 0)
        remote(csend.at[h], crecv.at[h], c_s.at[h], c_r.at[h], sibling).start()

        def own(n, carry):
            cols = pl.ds(pl.multiple_of(n * 256, 256), 256)
            pown[h, :, cols] = jnp.dot(sct[h, 0:256, :], act[:, cols], preferred_element_type=F32)
            return carry

        lax.fori_loop(0, 4, own, 0)

    def chip_sum():
        drain(crecv.at[0], c_r.at[0])

        def add(n, carry):
            rows = pl.ds(pl.multiple_of(n * 16, 16), 16)
            zsend[rows, :] = (pown[0, rows, :] + crecv[0, rows, :].astype(F32)).astype(BF16)
            return carry

        lax.fori_loop(0, 16, add, 0)

    for d in (1, 2, 3):
        drain(act.at[pl.ds(d * 256, 256)], act_r.at[d])
    arrived(0)
    exchange(2, 1)
    for d in range(4):
        scale(0, d)
    grad_down_part(0)
    for d in range(4):

        def back0(n, carry, d=d):
            part, cols = back_part(0, d, n)
            bp[d, :, cols] = part
            return carry

        lax.fori_loop(0, 4, back0, 0)
        if d == 0:
            chip_sum()

    for i in range(1, len(STAGES)):
        d = STAGES[i][1]
        arrived(i)
        if i + 2 < len(STAGES):
            exchange(i + 2, 1)
        for p in range(ZPARTS):
            if i == ZAT[p]:
                part = pl.ds(p * ZROWS, ZROWS)
                remote(zsend.at[part], zrecv.at[part], z_s.at[p], z_r.at[p], z_peer).start()
        scale(1, d)
        if d:

            def back1(n, carry, d=d):
                part, cols = back_part(1, d, n)
                bsend[d - 1, :, cols] = (bp[d, :, cols] + part).astype(BF16)
                return carry

            lax.fori_loop(0, 4, back1, 0)
            remote(
                bsend.at[d - 1], brecv.at[3 - d], b_s.at[d - 1], b_r.at[3 - d], at_x(d)
            ).start()
    grad_down_part(1)

    def back_own(n, carry):
        part, cols = back_part(1, 0, n)
        bp[0, :, cols] = bp[0, :, cols] + part
        return carry

    lax.fori_loop(0, 4, back_own, 0)

    for d in range(3):
        drain(brecv.at[d], b_r.at[d])

    def finish(i, carry):
        rows = pl.ds(pl.multiple_of(i * 16, 16), 16)
        back = bp[0, rows, :] + brecv[0, rows, :].astype(F32)
        back = back + brecv[1, rows, :].astype(F32) + brecv[2, rows, :].astype(F32)
        slot_grad = jnp.sum(act[rows, :].astype(F32) * back, axis=1, keepdims=True)
        sgb[rows, :] = jnp.broadcast_to(slot_grad, (16, 128))
        bp[0, rows, :] = wbuf[rows, 0:1].astype(F32) * back
        return carry

    lax.fori_loop(0, 16, finish, 0)

    pltpu.make_async_copy(wrows(sgb, e), wrows(ret, e), ret_r).start()

    def send_back(k, carry):
        to = (e + k) % ne
        remote(wrows(sgb, to), wrows(ret, e), ret_s, ret_r, (f, to)).start()
        return carry

    lax.fori_loop(1, ne, send_back, 0)

    def grad_pre(i, carry):
        rows = pl.ds(pl.multiple_of(i * 16, 16), 16)
        hidden = bp[0, rows, :]
        gp_out[rows, 0:1024] = (hidden * bvec[rows, 0:1024]).astype(BF16)
        gp_out[rows, 1024:2048] = (hidden * bvec[rows, 1024:2048]).astype(BF16)
        return carry

    lax.fori_loop(0, 16, grad_pre, 0)

    drain(crecv.at[1], c_r.at[1])

    def chip_total(n, carry):
        rows = pl.ds(pl.multiple_of(n * 16, 16), 16)
        pown[1, rows, :] = pown[1, rows, :] + crecv[1, rows, :].astype(F32)
        return carry

    lax.fori_loop(0, 16, chip_total, 0)

    def total(n, carry):
        rows = pl.ds(pl.multiple_of(n * 16, 16), 16)
        gd_out[rows, :] = pown[1, rows, :] + zrecv[rows, :].astype(F32)
        return carry


    drain(ret, ret_r)
    per_slot = (gbuf[0].astype(F32) * ret[...]).reshape(ne, CAP, 128)
    per_expert = jnp.sum(per_slot, axis=1)
    ids8 = meta[0, 0:8, :]
    dp = jnp.zeros((8, 128), F32)
    for k in range(ne):
        dp = dp + jnp.where(ids8 == float(k), per_expert[k : k + 1, :], 0.0)
    dp_out[...] = dp

    for p in range(ZPARTS):
        drain(zrecv.at[pl.ds(p * ZROWS, ZROWS)], z_r.at[p])
        lax.fori_loop(p * ZROWS // 16, (p + 1) * ZROWS // 16, total, 0)

    for d in (1, 2, 3):
        drain(meta.at[0], meta_s.at[d])
        for h in range(2):
            drain(ogb.at[0, h], og_s.at[h, d])
        drain(act.at[pl.ds(0, 256)], act_s.at[d])
        drain(bsend.at[0], b_s.at[d - 1])
    for i in range(3):
        drain(wq.at[0, pl.ds(0, 256), :], w_s.at[i])
    for h in range(2):
        drain(csend.at[h], c_s.at[h])
    for p in range(ZPARTS):
        drain(zsend.at[pl.ds(p * ZROWS, ZROWS)], z_s.at[p])
    for i, (h, d0, dn) in enumerate(STAGES):
        drain(sendbuf.at[h, pl.ds(d0, dn), pl.ds(0, (ne - 1) * CAP), :], a_s.at[i])
    drain(wsend.at[pl.ds(0, (ne - 1) * CAP)], a_s.at[WSTAGE])
    drain(sgb.at[pl.ds(0, (ne - 1) * CAP)], ret_s)


def write_out(dp, gp, gd, dp_out, gp_out, gd_out, sem):
    copies = [
        pltpu.make_async_copy(src, dst, sem.at[i])
        for i, (src, dst) in enumerate(((gp, gp_out), (gd, gd_out), (dp, dp_out)))
    ]
    for copy in copies:
        copy.start()
    for copy in copies:
        copy.wait()


def per_device(out_grad, router_probs, expert_ids, saved_hidden, w_down):
    dma = pltpu.SemaphoreType.DMA
    vmem = pl.BlockSpec(memory_space=pltpu.VMEM)
    hbm = pl.BlockSpec(memory_space=pl.ANY)
    stages = len(STAGES) + 1
    dp, gp, gd = pl.pallas_call(
        kernel,
        out_shape=(
            pltpu.VMEM((8, 128), F32),
            pltpu.VMEM((256, 2048), BF16),
            pltpu.VMEM((256, 1024), F32),
        ),
        in_specs=[hbm] * 5,
        out_specs=(vmem, vmem, vmem),
        scratch_shapes=[
            pltpu.VMEM((4, 16, 128), F32),
            pltpu.VMEM((4, 2, 128, 512), BF16),
            pltpu.VMEM((4, 256, 128), BF16),
            pltpu.VMEM((256, 128), BF16),
            pltpu.VMEM((256, 128), BF16),
            pltpu.VMEM((2, 4, 256, 512), BF16),
            pltpu.VMEM((2, 4, 256, 512), BF16),
            pltpu.VMEM((256, 2048), BF16),
            pltpu.VMEM((1024, 1024), BF16),
            pltpu.VMEM((256, 2048), F32),
            pltpu.VMEM((2, 512, 1024), BF16),
            pltpu.VMEM((2, 512, 1024), BF16),
            pltpu.VMEM((2, 256, 1024), F32),
            pltpu.VMEM((2, 256, 1024), BF16),
            pltpu.VMEM((2, 256, 1024), BF16),
            pltpu.VMEM((256, 1024), BF16),
            pltpu.VMEM((256, 1024), BF16),
            pltpu.VMEM((4, 256, 1024), F32),
            pltpu.VMEM((3, 256, 1024), BF16),
            pltpu.VMEM((3, 256, 1024), BF16),
            pltpu.VMEM((256, 128), F32),
            pltpu.VMEM((256, 128), F32),
            pltpu.VMEM((8, 128), jnp.int32),
            pltpu.VMEM((8, 128), BF16),
            dma((2,)),
            dma,
            dma((4,)), dma((4,)),
            dma((2, 4)), dma((2, 4)),
            dma((3,)), dma((4,)),
            dma((4,)), dma((4,)),
            dma((stages,)), dma((stages,)),
            dma((2,)), dma((2,)),
            dma((ZPARTS,)), dma((ZPARTS,)),
            dma((3,)), dma((3,)),
            dma, dma,
        ],
        compiler_params=pltpu.CompilerParams(
            collective_id=0, has_side_effects=True, vmem_limit_bytes=56 * 2**20
        ),
    )(
        expert_ids.T,
        router_probs.T,
        out_grad,
        saved_hidden.reshape(256, 2048),
        w_down.reshape(256, 1024),
    )
    dp, gp, gd = pl.pallas_call(
        write_out,
        out_shape=(
            jax.ShapeDtypeStruct((8, 128), F32),
            jax.ShapeDtypeStruct((256, 2048), BF16),
            jax.ShapeDtypeStruct((256, 1024), F32),
        ),
        in_specs=[hbm] * 3,
        out_specs=(hbm,) * 3,
        scratch_shapes=[dma((3,))],
    )(*(pltpu.with_memory_space_constraint(v, pltpu.VMEM) for v in (dp, gp, gd)))
    return dp.T, gp.reshape(1, 1, 256, 2048), gd.reshape(1, 256, 1024)


def solution(mesh):
    placed = (
        P(("fsdp", "expert"), None),
        P(("fsdp", "expert"), None),
        P(("fsdp", "expert"), None),
        P("fsdp", "expert", None, None),
        P("expert", "fsdp", None),
    )
    return jax.shard_map(
        per_device,
        mesh=mesh,
        in_specs=placed,
        out_specs=(
            P(("fsdp", "expert"), None),
            P("fsdp", "expert", None, None),
            P("expert", "fsdp", None),
        ),
        check_vma=False,
    )
```

```python
import jax
import jax.numpy as jnp
from jax import lax
from jax.experimental import pallas as pl
from jax.experimental.pallas import tpu as pltpu
from jax.sharding import PartitionSpec as P

F32 = jnp.float32
BF16 = jnp.bfloat16
MESH = pl.DeviceIdType.MESH
CAP = 16
NX = 4
STAGES = ((0, 1, 3), (1, 2, 1), (1, 1, 1), (1, 3, 1), (0, 0, 1), (1, 0, 1))
WSTAGE = len(STAGES)
ISSUE = ((1, 5), (6, 0), (6, 0))
ZPARTS = 8
ZFIRST = 5
ZROWS = 256 // ZPARTS


def kernel(
    ids_hbm, probs_hbm, og_hbm, hid_hbm, w_hbm,
    dp_out, gp_out, gd_out,
    meta, ogb, gbuf, wsend, wbuf, sendbuf, routed, hidv, act, bvec, wq, sct, pown,
    csend, crecv, zsend, zrecv, bp, bsend, brecv, sgb, ret,
    ids_ref, probs_ref, in_sem, hid_sem, meta_s, meta_r, og_s, og_r, w_s, w_r, act_s, act_r, a_s, a_r,
    c_s, c_r, z_s, z_r, b_s, b_r, ret_s, ret_r,
    acth, wswap, bgive, btake, as_s, as_r, ws_s, ws_r, bs_s, bs_r,
):
    ne = 16
    f = lax.axis_index("fsdp")
    e = lax.axis_index("expert")
    zh, x, c = f // 8, (f // 2) % 4, f % 2
    zl, y = e // 4, e % 4

    def at_x(d):
        return (zh * 8 + ((x + d) % 4) * 2 + c, e)

    z_peer = ((1 - zh) * 8 + x * 2 + c, e)
    sibling = (zh * 8 + x * 2 + 1 - c, e)

    def away(to):
        gap = (zl - to // 4) * (zl - to // 4)
        return gap // 9 + ((gap // 4) % 2) * ((y + to % 4) % 2)

    def near(to):
        return (((zh + away(to)) % 2) * 8 + x * 2 + c, to)

    def for_away(do):
        def one(to, carry):
            @pl.when(away(to) == 1)
            def _():
                do(to)

            return carry

        lax.fori_loop(0, ne, one, 0)

    def remote(src, dst, ss, rs, dev):
        return pltpu.make_async_remote_copy(
            src_ref=src, dst_ref=dst, send_sem=ss, recv_sem=rs, device_id=dev, device_id_type=MESH
        )

    def drain(ref, sem):
        pltpu.make_async_copy(ref, ref, sem).wait()

    own_w = pltpu.make_async_copy(w_hbm, wq.at[1, pl.ds(0, 256), :], w_r.at[0])
    own_hid = pltpu.make_async_copy(hid_hbm, hidv, hid_sem)

    def og_columns(xt, h):
        col = ((zh + 1 - h) % 2) * 2048 + xt * 512
        return og_hbm.at[:, pl.ds(pl.multiple_of(col, 512), 512)]

    barrier = pltpu.get_barrier_semaphore()
    for d in (1, 2, 3):
        pl.semaphore_signal(barrier, inc=1, device_id=at_x(d), device_id_type=MESH)
    pl.semaphore_signal(barrier, inc=1, device_id=z_peer, device_id_type=MESH)
    pl.semaphore_signal(barrier, inc=1, device_id=sibling, device_id_type=MESH)

    def greet(k, carry):
        to = (e + k) % ne
        pl.semaphore_signal(barrier, inc=1, device_id=near(to), device_id_type=MESH)

        @pl.when(away(to) == 1)
        def _():
            pl.semaphore_signal(barrier, inc=1, device_id=(f, to), device_id_type=MESH)

        return carry + away(to)

    extra = lax.fori_loop(1, ne, greet, 0)
    for h in range(2):
        pltpu.make_async_copy(og_columns(x, h), ogb.at[0, h], og_r.at[h, 0]).start()
    own_hid.start()
    own_w.start()
    own_ids = pltpu.make_async_copy(ids_hbm, ids_ref, in_sem.at[0])
    own_probs = pltpu.make_async_copy(probs_hbm, probs_ref, in_sem.at[1])
    own_ids.start()
    own_probs.start()
    own_ids.wait()
    own_probs.wait()
    meta[0, 0:8, :] = ids_ref[...].astype(F32)
    meta[0, 8:16, :] = probs_ref[...].astype(F32)

    own_hid.wait()

    def wrows(ref, who):
        return ref.at[pl.ds(pl.multiple_of(who * CAP, CAP), CAP), :]

    def activate(i, carry):
        rows = pl.ds(pl.multiple_of(i * CAP, CAP), CAP)
        gate = hidv[rows, 0:1024].astype(F32)
        up = hidv[rows, 1024:2048].astype(F32)
        sigma = jax.nn.sigmoid(gate)
        silu = gate * sigma
        bvec[rows, 0:1024] = up * sigma * (1.0 + gate * (1.0 - sigma))
        bvec[rows, 1024:2048] = silu
        value = (silu * up).astype(BF16)
        acth[rows, :] = value

        @pl.when(away(i) == 0)
        def _():
            act[rows, :] = value

        return carry

    lax.fori_loop(0, ne, activate, 0)
    pl.semaphore_wait(barrier, 5 + ne - 1 + extra)
    for_away(
        lambda to: remote(
            wrows(acth, to), wrows(act, to), as_s.at[to], as_r.at[to], z_peer
        ).start()
    )

    for d in (2, 1, 3):
        remote(meta.at[0], meta.at[4 - d], meta_s.at[d], meta_r.at[4 - d], at_x(d)).start()
    for h in range(2):
        for d in (2, 1, 3):
            remote(
                og_columns((x + d) % 4, h),
                ogb.at[4 - d, h],
                og_s.at[h, d],
                og_r.at[h, 4 - d],
                at_x(d),
            ).start()
        if h == 0:
            remote(w_hbm, wq.at[0, pl.ds(0, 256), :], w_s.at[0], w_r.at[1], z_peer).start()
            remote(w_hbm, wq.at[1, pl.ds(256, 256), :], w_s.at[1], w_r.at[2], sibling).start()

    tri_r = lax.broadcasted_iota(jnp.int32, (128, 128), 0)
    tri_c = lax.broadcasted_iota(jnp.int32, (128, 128), 1)
    upper = jnp.where(tri_r < tri_c, 1.0, 0.0).astype(BF16)
    e_iota = lax.broadcasted_iota(jnp.int32, (ne, 128), 0).astype(F32)
    r_iota = lax.broadcasted_iota(jnp.int32, (ne, CAP, 128), 1).astype(F32)
    lane = lax.broadcasted_iota(jnp.int32, (ne * CAP, 128), 1)
    wacc = jnp.zeros((ne * CAP, 128), F32)
    for d in (0, 1, 3, 2):
        if d:
            drain(meta.at[d], meta_r.at[d])
        ids8 = meta[d, 0:8, :]
        pr8 = meta[d, 8:16, :]
        named = jnp.zeros((ne, 128), F32)
        prob = jnp.zeros((ne, 128), F32)
        for k in range(8):
            hit = ids8[k : k + 1, :] == e_iota
            named = named + jnp.where(hit, 1.0, 0.0)
            prob = prob + jnp.where(hit, pr8[k : k + 1, :], 0.0)
        rank = jnp.dot(named.astype(BF16), upper, preferred_element_type=F32)
        rank = jnp.where(named > 0.0, rank, -1.0)
        pick = jnp.where(rank[:, None, :] == r_iota, 1.0, 0.0)
        wcol = jnp.sum((pick * prob[:, None, :]).reshape(ne * CAP, 128), axis=1, keepdims=True)
        wacc = jnp.where(lane == d, wcol, wacc)
        gbuf[d] = pick.reshape(ne * CAP, 128).astype(BF16)
    wsend[...] = wacc.astype(BF16)

    def expand(h):
        for d in (0, 1, 3, 2):
            drain(ogb.at[d, h], og_r.at[h, d])
            for dc in range(2):
                columns = pl.ds(pl.multiple_of(((c + dc) % 2) * 256, 256), 256)
                sendbuf[h, d, :, dc * 256 : dc * 256 + 256] = jnp.dot(
                    gbuf[d], ogb[d, h, :, columns], preferred_element_type=F32
                ).astype(BF16)

    def my_rows(ref, h, d0, dn, who):
        return ref.at[h, pl.ds(d0, dn), pl.ds(pl.multiple_of(who * CAP, CAP), CAP), :]

    def exchange(first, count):
        for i in range(first, first + count):
            h, d0, dn = STAGES[i]
            pltpu.make_async_copy(
                my_rows(sendbuf, h, d0, dn, e), my_rows(routed, h, d0, dn, e), a_r.at[i]
            ).start()

            def send(k, carry):
                to = (e + k) % ne
                remote(
                    my_rows(sendbuf, (h + away(to)) % 2, d0, dn, to),
                    my_rows(routed, h, d0, dn, e),
                    a_s.at[i],
                    a_r.at[i],
                    near(to),
                ).start()
                return carry

            lax.fori_loop(1, ne, send, 0)

    def arrived(i):
        h, d0, dn = STAGES[i]
        drain(routed.at[h, pl.ds(d0, dn)], a_r.at[i])

    pltpu.make_async_copy(wrows(wsend, e), wrows(wbuf, e), a_r.at[WSTAGE]).start()

    def send_weight(k, carry):
        to = (e + k) % ne
        remote(
            wrows(wsend, to), wrows(wbuf, e), a_s.at[WSTAGE], a_r.at[WSTAGE], near(to)
        ).start()
        return carry

    lax.fori_loop(1, ne, send_weight, 0)
    expand(0)
    expand(1)
    exchange(0, 1)
    exchange(*ISSUE[0])

    for_away(lambda to: drain(wrows(act, to), as_r.at[to]))
    for d in (2, 1, 3):
        remote(
            act.at[pl.ds(0, 256)],
            act.at[pl.ds((4 - d) * 256, 256)],
            act_s.at[d],
            act_r.at[4 - d],
            at_x(d),
        ).start()

    drain(wq.at[0, pl.ds(0, 256), :], w_r.at[1])
    remote(
        wq.at[0, pl.ds(0, 256), :], wq.at[0, pl.ds(256, 256), :], w_s.at[2], w_r.at[3], sibling
    ).start()
    drain(wbuf, a_r.at[WSTAGE])
    for_away(
        lambda to: remote(
            wrows(wbuf, to), wrows(wswap, to), ws_s.at[to], ws_r.at[to], z_peer
        ).start()
    )
    own_w.wait()
    drain(wq.at[1, pl.ds(256, 256), :], w_r.at[2])
    drain(wq.at[0, pl.ds(256, 256), :], w_r.at[3])

    def scale(h, d):
        wcol = wbuf[:, d : d + 1].astype(F32)
        for b in range(4):
            part = routed[h, d, :, b * 128 : b * 128 + 128].astype(F32) * wcol
            sct[h, b * 128 : b * 128 + 128, d * 256 : d * 256 + 256] = part.T.astype(BF16)

    def back_part(h, d, n):
        cols = pl.ds(pl.multiple_of(n * 256, 256), 256)
        return jnp.dot(routed[h, d], wq[h, :, cols], preferred_element_type=F32), cols

    def grad_down_part(h):
        def sib(n, carry):
            cols = pl.ds(pl.multiple_of(n * 256, 256), 256)
            csend[h, :, cols] = jnp.dot(
                sct[h, 256:512, :], act[:, cols], preferred_element_type=F32
            ).astype(BF16)
            return carry

        lax.fori_loop(0, 4, sib, 0)
        remote(csend.at[h], crecv.at[h], c_s.at[h], c_r.at[h], sibling).start()

        def own(n, carry):
            cols = pl.ds(pl.multiple_of(n * 256, 256), 256)
            pown[h, :, cols] = jnp.dot(sct[h, 0:256, :], act[:, cols], preferred_element_type=F32)
            return carry

        lax.fori_loop(0, 4, own, 0)

    def chip_sum():
        drain(crecv.at[0], c_r.at[0])

        def add(n, carry):
            rows = pl.ds(pl.multiple_of(n * 16, 16), 16)
            zsend[rows, :] = (pown[0, rows, :] + crecv[0, rows, :].astype(F32)).astype(BF16)
            return carry

        lax.fori_loop(0, 16, add, 0)

    def back_first(d):
        def one(n, carry):
            part, cols = back_part(0, d, n)
            bp[d, :, cols] = part
            return carry

        lax.fori_loop(0, 4, one, 0)

    def back_second(d):
        def one(n, carry):
            part, cols = back_part(1, d, n)
            if d:
                bsend[d - 1, :, cols] = (bp[d, :, cols] + part).astype(BF16)
            else:
                bp[0, :, cols] = bp[0, :, cols] + part
            return carry

        lax.fori_loop(0, 4, one, 0)
        if d:
            remote(
                bsend.at[d - 1], brecv.at[3 - d], b_s.at[d - 1], b_r.at[3 - d], at_x(d)
            ).start()

    def start_z(p):
        part = pl.ds(p * ZROWS, ZROWS)
        remote(zsend.at[part], zrecv.at[part], z_s.at[p], z_r.at[p], z_peer).start()

    arrived(0)
    exchange(*ISSUE[1])
    for d in (2, 1, 3):
        back_first(d)
    arrived(1)
    exchange(*ISSUE[2])
    back_second(2)
    arrived(2)
    back_second(1)
    arrived(3)
    back_second(3)
    for d in (1, 2, 3):
        drain(act.at[pl.ds(d * 256, 256)], act_r.at[d])
    for d in (2, 1, 3):
        scale(0, d)
    arrived(4)
    scale(0, 0)
    grad_down_part(0)
    for d in (2, 1, 3):
        scale(1, d)
    chip_sum()
    arrived(5)
    for p in range(ZFIRST):
        start_z(p)
    scale(1, 0)
    grad_down_part(1)
    back_first(0)
    back_second(0)

    for d in range(3):
        drain(brecv.at[d], b_r.at[d])

    def sum_x(i, carry):
        rows = pl.ds(pl.multiple_of(i * CAP, CAP), CAP)
        back = bp[0, rows, :] + brecv[0, rows, :].astype(F32)
        back = back + brecv[1, rows, :].astype(F32) + brecv[2, rows, :].astype(F32)
        bp[0, rows, :] = back

        @pl.when(away(i) == 1)
        def _():
            bgive[rows, :] = back.astype(BF16)
            remote(
                wrows(bgive, i), wrows(btake, i), bs_s.at[i], bs_r.at[i], z_peer
            ).start()

        return carry

    lax.fori_loop(0, ne, sum_x, 0)
    for p in range(ZFIRST, ZPARTS):
        start_z(p)

    def take(to):
        rows = pl.ds(pl.multiple_of(to * CAP, CAP), CAP)
        drain(wrows(btake, to), bs_r.at[to])
        drain(wrows(wswap, to), ws_r.at[to])
        bp[0, rows, :] = btake[rows, :].astype(F32)

    def finish(i, carry):
        rows = pl.ds(pl.multiple_of(i * CAP, CAP), CAP)
        back = bp[0, rows, :]
        slot_grad = jnp.sum(acth[rows, :].astype(F32) * back, axis=1, keepdims=True)
        sgb[rows, :] = jnp.broadcast_to(slot_grad, (16, 128))
        weight = jnp.where(away(i) == 1, wswap[rows, 0:1].astype(F32), wbuf[rows, 0:1].astype(F32))
        bp[0, rows, :] = weight * back
        return carry

    for_away(take)
    lax.fori_loop(0, ne, finish, 0)

    pltpu.make_async_copy(wrows(sgb, e), wrows(ret, e), ret_r).start()

    def send_back(k, carry):
        to = (e + k) % ne
        remote(wrows(sgb, to), wrows(ret, e), ret_s, ret_r, (f, to)).start()
        return carry

    lax.fori_loop(1, ne, send_back, 0)

    def grad_pre(i, carry):
        rows = pl.ds(pl.multiple_of(i * 16, 16), 16)
        hidden = bp[0, rows, :]
        gp_out[rows, 0:1024] = (hidden * bvec[rows, 0:1024]).astype(BF16)
        gp_out[rows, 1024:2048] = (hidden * bvec[rows, 1024:2048]).astype(BF16)
        return carry

    lax.fori_loop(0, 16, grad_pre, 0)

    drain(crecv.at[1], c_r.at[1])

    def chip_total(n, carry):
        rows = pl.ds(pl.multiple_of(n * 16, 16), 16)
        pown[1, rows, :] = pown[1, rows, :] + crecv[1, rows, :].astype(F32)
        return carry

    lax.fori_loop(0, 16, chip_total, 0)

    def total(n, carry):
        rows = pl.ds(pl.multiple_of(n * 16, 16), 16)
        gd_out[rows, :] = pown[1, rows, :] + zrecv[rows, :].astype(F32)
        return carry


    drain(ret, ret_r)
    per_slot = (gbuf[0].astype(F32) * ret[...]).reshape(ne, CAP, 128)
    per_expert = jnp.sum(per_slot, axis=1)
    ids8 = meta[0, 0:8, :]
    dp = jnp.zeros((8, 128), F32)
    for k in range(ne):
        dp = dp + jnp.where(ids8 == float(k), per_expert[k : k + 1, :], 0.0)
    dp_out[...] = dp

    for p in range(ZPARTS):
        drain(zrecv.at[pl.ds(p * ZROWS, ZROWS)], z_r.at[p])
        lax.fori_loop(p * ZROWS // 16, (p + 1) * ZROWS // 16, total, 0)

    def left(to):
        drain(wrows(acth, to), as_s.at[to])
        drain(wrows(wbuf, to), ws_s.at[to])
        drain(wrows(bgive, to), bs_s.at[to])

    for_away(left)
    for d in (1, 2, 3):
        drain(meta.at[0], meta_s.at[d])
        for h in range(2):
            drain(ogb.at[0, h], og_s.at[h, d])
        drain(act.at[pl.ds(0, 256)], act_s.at[d])
        drain(bsend.at[0], b_s.at[d - 1])
    for i in range(3):
        drain(wq.at[0, pl.ds(0, 256), :], w_s.at[i])
    for h in range(2):
        drain(csend.at[h], c_s.at[h])
    for p in range(ZPARTS):
        drain(zsend.at[pl.ds(p * ZROWS, ZROWS)], z_s.at[p])
    for i, (h, d0, dn) in enumerate(STAGES):
        drain(sendbuf.at[h, pl.ds(d0, dn), pl.ds(0, (ne - 1) * CAP), :], a_s.at[i])
    drain(wsend.at[pl.ds(0, (ne - 1) * CAP)], a_s.at[WSTAGE])
    drain(sgb.at[pl.ds(0, (ne - 1) * CAP)], ret_s)


def write_out(dp, gp, gd, dp_out, gp_out, gd_out, sem):
    copies = [
        pltpu.make_async_copy(src, dst, sem.at[i])
        for i, (src, dst) in enumerate(((gp, gp_out), (gd, gd_out), (dp, dp_out)))
    ]
    for copy in copies:
        copy.start()
    for copy in copies:
        copy.wait()


def per_device(out_grad, router_probs, expert_ids, saved_hidden, w_down):
    dma = pltpu.SemaphoreType.DMA
    vmem = pl.BlockSpec(memory_space=pltpu.VMEM)
    hbm = pl.BlockSpec(memory_space=pl.ANY)
    stages = len(STAGES) + 1
    dp, gp, gd = pl.pallas_call(
        kernel,
        out_shape=(
            pltpu.VMEM((8, 128), F32),
            pltpu.VMEM((256, 2048), BF16),
            pltpu.VMEM((256, 1024), F32),
        ),
        in_specs=[hbm] * 5,
        out_specs=(vmem, vmem, vmem),
        scratch_shapes=[
            pltpu.VMEM((4, 16, 128), F32),
            pltpu.VMEM((4, 2, 128, 512), BF16),
            pltpu.VMEM((4, 256, 128), BF16),
            pltpu.VMEM((256, 128), BF16),
            pltpu.VMEM((256, 128), BF16),
            pltpu.VMEM((2, 4, 256, 512), BF16),
            pltpu.VMEM((2, 4, 256, 512), BF16),
            pltpu.VMEM((256, 2048), BF16),
            pltpu.VMEM((1024, 1024), BF16),
            pltpu.VMEM((256, 2048), F32),
            pltpu.VMEM((2, 512, 1024), BF16),
            pltpu.VMEM((2, 512, 1024), BF16),
            pltpu.VMEM((2, 256, 1024), F32),
            pltpu.VMEM((2, 256, 1024), BF16),
            pltpu.VMEM((2, 256, 1024), BF16),
            pltpu.VMEM((256, 1024), BF16),
            pltpu.VMEM((256, 1024), BF16),
            pltpu.VMEM((4, 256, 1024), F32),
            pltpu.VMEM((3, 256, 1024), BF16),
            pltpu.VMEM((3, 256, 1024), BF16),
            pltpu.VMEM((256, 128), F32),
            pltpu.VMEM((256, 128), F32),
            pltpu.VMEM((8, 128), jnp.int32),
            pltpu.VMEM((8, 128), BF16),
            dma((2,)),
            dma,
            dma((4,)), dma((4,)),
            dma((2, 4)), dma((2, 4)),
            dma((3,)), dma((4,)),
            dma((4,)), dma((4,)),
            dma((stages,)), dma((stages,)),
            dma((2,)), dma((2,)),
            dma((ZPARTS,)), dma((ZPARTS,)),
            dma((3,)), dma((3,)),
            dma, dma,
            pltpu.VMEM((256, 1024), BF16),
            pltpu.VMEM((256, 128), BF16),
            pltpu.VMEM((256, 1024), BF16),
            pltpu.VMEM((256, 1024), BF16),
            dma((16,)), dma((16,)),
            dma((16,)), dma((16,)),
            dma((16,)), dma((16,)),
        ],
        compiler_params=pltpu.CompilerParams(
            collective_id=0, has_side_effects=True, vmem_limit_bytes=56 * 2**20
        ),
    )(
        expert_ids.T,
        router_probs.T,
        out_grad,
        saved_hidden.reshape(256, 2048),
        w_down.reshape(256, 1024),
    )
    dp, gp, gd = pl.pallas_call(
        write_out,
        out_shape=(
            jax.ShapeDtypeStruct((8, 128), F32),
            jax.ShapeDtypeStruct((256, 2048), BF16),
            jax.ShapeDtypeStruct((256, 1024), F32),
        ),
        in_specs=[hbm] * 3,
        out_specs=(hbm,) * 3,
        scratch_shapes=[dma((3,))],
    )(*(pltpu.with_memory_space_constraint(v, pltpu.VMEM) for v in (dp, gp, gd)))
    return dp.T, gp.reshape(1, 1, 256, 2048), gd.reshape(1, 256, 1024)


def solution(mesh):
    placed = (
        P(("fsdp", "expert"), None),
        P(("fsdp", "expert"), None),
        P(("fsdp", "expert"), None),
        P("fsdp", "expert", None, None),
        P("expert", "fsdp", None),
    )
    return jax.shard_map(
        per_device,
        mesh=mesh,
        in_specs=placed,
        out_specs=(
            P(("fsdp", "expert"), None),
            P("fsdp", "expert", None, None),
            P("expert", "fsdp", None),
        ),
        check_vma=False,
    )
```

```python
import jax
import jax.numpy as jnp
from jax import lax
from jax.experimental import pallas as pl
from jax.experimental.pallas import tpu as pltpu
from jax.sharding import PartitionSpec as P

F32 = jnp.float32
BF16 = jnp.bfloat16
MESH = pl.DeviceIdType.MESH
CAP = 16
NX = 4
STAGES = ((0, 1, 3), (1, 2, 1), (1, 1, 1), (1, 3, 1), (0, 0, 1), (1, 0, 1))
WSTAGE = len(STAGES)
ISSUE = ((1, 5), (6, 0), (6, 0))
ZPARTS = 8
ZFIRST = 5
ZROWS = 256 // ZPARTS


def kernel(
    ids_hbm, probs_hbm, og_hbm, hid_hbm, w_hbm,
    dp_out, gp_out, gd_out,
    meta, ogb, gbuf, wsend, wbuf, sendbuf, routed, hidv, act, bvec, wq, sct, pown,
    csend, crecv, zsend, zrecv, bp, bsend, brecv, sgb, ret,
    ids_ref, probs_ref, in_sem, hid_sem, meta_s, meta_r, og_s, og_r, w_s, w_r, act_s, act_r, a_s, a_r,
    c_s, c_r, z_s, z_r, b_s, b_r, ret_s, ret_r,
    acth, wswap, bgive, btake, as_s, as_r, ws_s, ws_r, bs_s, bs_r,
):
    ne = 16
    f = lax.axis_index("fsdp")
    e = lax.axis_index("expert")
    zh, x, c = f // 8, (f // 2) % 4, f % 2
    zl, y = e // 4, e % 4

    def at_x(d):
        return (zh * 8 + ((x + d) % 4) * 2 + c, e)

    z_peer = ((1 - zh) * 8 + x * 2 + c, e)
    sibling = (zh * 8 + x * 2 + 1 - c, e)

    def away(to):
        gap = (zl - to // 4) * (zl - to // 4)
        return gap // 9 + ((gap // 4) % 2) * ((y + to % 4) % 2)

    def near(to):
        return (((zh + away(to)) % 2) * 8 + x * 2 + c, to)

    def for_away(do):
        def one(to, carry):
            @pl.when(away(to) == 1)
            def _():
                do(to)

            return carry

        lax.fori_loop(0, ne, one, 0)

    def remote(src, dst, ss, rs, dev):
        return pltpu.make_async_remote_copy(
            src_ref=src, dst_ref=dst, send_sem=ss, recv_sem=rs, device_id=dev, device_id_type=MESH
        )

    def drain(ref, sem):
        pltpu.make_async_copy(ref, ref, sem).wait()

    own_w = pltpu.make_async_copy(w_hbm, wq.at[1, pl.ds(0, 256), :], w_r.at[0])
    own_hid = pltpu.make_async_copy(hid_hbm, hidv, hid_sem)

    def og_columns(xt, h):
        col = ((zh + 1 - h) % 2) * 2048 + xt * 512
        return og_hbm.at[:, pl.ds(pl.multiple_of(col, 512), 512)]

    barrier = pltpu.get_barrier_semaphore()
    for d in (1, 2, 3):
        pl.semaphore_signal(barrier, inc=1, device_id=at_x(d), device_id_type=MESH)
    pl.semaphore_signal(barrier, inc=1, device_id=z_peer, device_id_type=MESH)
    pl.semaphore_signal(barrier, inc=1, device_id=sibling, device_id_type=MESH)

    def greet(k, carry):
        to = (e + k) % ne
        pl.semaphore_signal(barrier, inc=1, device_id=near(to), device_id_type=MESH)

        @pl.when(away(to) == 1)
        def _():
            pl.semaphore_signal(barrier, inc=1, device_id=(f, to), device_id_type=MESH)

        return carry + away(to)

    extra = lax.fori_loop(1, ne, greet, 0)
    for h in range(2):
        pltpu.make_async_copy(og_columns(x, h), ogb.at[0, h], og_r.at[h, 0]).start()
    own_hid.start()
    own_w.start()
    own_ids = pltpu.make_async_copy(ids_hbm, ids_ref, in_sem.at[0])
    own_probs = pltpu.make_async_copy(probs_hbm, probs_ref, in_sem.at[1])
    own_ids.start()
    own_probs.start()
    own_ids.wait()
    own_probs.wait()
    meta[0, 0:8, :] = ids_ref[...].astype(F32)
    meta[0, 8:16, :] = probs_ref[...].astype(F32)

    own_hid.wait()

    def wrows(ref, who):
        return ref.at[pl.ds(pl.multiple_of(who * CAP, CAP), CAP), :]

    def activate(i, carry):
        rows = pl.ds(pl.multiple_of(i * CAP, CAP), CAP)
        gate = hidv[rows, 0:1024].astype(F32)
        up = hidv[rows, 1024:2048].astype(F32)
        sigma = jax.nn.sigmoid(gate)
        silu = gate * sigma
        bvec[rows, 0:1024] = up * sigma * (1.0 + gate * (1.0 - sigma))
        bvec[rows, 1024:2048] = silu
        value = (silu * up).astype(BF16)
        acth[rows, :] = value

        @pl.when(away(i) == 0)
        def _():
            act[rows, :] = value

        return carry

    lax.fori_loop(0, ne, activate, 0)
    pl.semaphore_wait(barrier, 5 + ne - 1 + extra)
    for_away(
        lambda to: remote(
            wrows(acth, to), wrows(act, to), as_s.at[to], as_r.at[to], z_peer
        ).start()
    )

    for d in (2, 1, 3):
        remote(meta.at[0], meta.at[4 - d], meta_s.at[d], meta_r.at[4 - d], at_x(d)).start()
    for h in range(2):
        for d in (2, 1, 3):
            remote(
                og_columns((x + d) % 4, h),
                ogb.at[4 - d, h],
                og_s.at[h, d],
                og_r.at[h, 4 - d],
                at_x(d),
            ).start()
        if h == 0:
            remote(w_hbm, wq.at[0, pl.ds(0, 256), :], w_s.at[0], w_r.at[1], z_peer).start()
            remote(w_hbm, wq.at[1, pl.ds(256, 256), :], w_s.at[1], w_r.at[2], sibling).start()

    tri_r = lax.broadcasted_iota(jnp.int32, (128, 128), 0)
    tri_c = lax.broadcasted_iota(jnp.int32, (128, 128), 1)
    upper = jnp.where(tri_r < tri_c, 1.0, 0.0).astype(BF16)
    e_iota = lax.broadcasted_iota(jnp.int32, (ne, 128), 0).astype(F32)
    r_iota = lax.broadcasted_iota(jnp.int32, (ne, CAP, 128), 1).astype(F32)
    lane = lax.broadcasted_iota(jnp.int32, (ne * CAP, 128), 1)
    wacc = jnp.zeros((ne * CAP, 128), F32)
    for d in (0, 1, 3, 2):
        if d:
            drain(meta.at[d], meta_r.at[d])
        ids8 = meta[d, 0:8, :]
        pr8 = meta[d, 8:16, :]
        named = jnp.zeros((ne, 128), F32)
        prob = jnp.zeros((ne, 128), F32)
        for k in range(8):
            hit = ids8[k : k + 1, :] == e_iota
            named = named + jnp.where(hit, 1.0, 0.0)
            prob = prob + jnp.where(hit, pr8[k : k + 1, :], 0.0)
        rank = jnp.dot(named.astype(BF16), upper, preferred_element_type=F32)
        rank = jnp.where(named > 0.0, rank, -1.0)
        pick = jnp.where(rank[:, None, :] == r_iota, 1.0, 0.0)
        wcol = jnp.sum((pick * prob[:, None, :]).reshape(ne * CAP, 128), axis=1, keepdims=True)
        wacc = jnp.where(lane == d, wcol, wacc)
        gbuf[d] = pick.reshape(ne * CAP, 128).astype(BF16)
    wsend[...] = wacc.astype(BF16)

    for_away(lambda to: drain(wrows(act, to), as_r.at[to]))
    for d in (2, 1, 3):
        remote(
            act.at[pl.ds(0, 256)],
            act.at[pl.ds((4 - d) * 256, 256)],
            act_s.at[d],
            act_r.at[4 - d],
            at_x(d),
        ).start()

    def expand(h):
        for d in (0, 1, 3, 2):
            drain(ogb.at[d, h], og_r.at[h, d])
            for dc in range(2):
                columns = pl.ds(pl.multiple_of(((c + dc) % 2) * 256, 256), 256)
                sendbuf[h, d, :, dc * 256 : dc * 256 + 256] = jnp.dot(
                    gbuf[d], ogb[d, h, :, columns], preferred_element_type=F32
                ).astype(BF16)

    def my_rows(ref, h, d0, dn, who):
        return ref.at[h, pl.ds(d0, dn), pl.ds(pl.multiple_of(who * CAP, CAP), CAP), :]

    def exchange(first, count):
        for i in range(first, first + count):
            h, d0, dn = STAGES[i]
            pltpu.make_async_copy(
                my_rows(sendbuf, h, d0, dn, e), my_rows(routed, h, d0, dn, e), a_r.at[i]
            ).start()

            def send(k, carry):
                to = (e + k) % ne
                remote(
                    my_rows(sendbuf, (h + away(to)) % 2, d0, dn, to),
                    my_rows(routed, h, d0, dn, e),
                    a_s.at[i],
                    a_r.at[i],
                    near(to),
                ).start()
                return carry

            lax.fori_loop(1, ne, send, 0)

    def arrived(i):
        h, d0, dn = STAGES[i]
        drain(routed.at[h, pl.ds(d0, dn)], a_r.at[i])

    pltpu.make_async_copy(wrows(wsend, e), wrows(wbuf, e), a_r.at[WSTAGE]).start()

    def send_weight(k, carry):
        to = (e + k) % ne
        remote(
            wrows(wsend, to), wrows(wbuf, e), a_s.at[WSTAGE], a_r.at[WSTAGE], near(to)
        ).start()
        return carry

    lax.fori_loop(1, ne, send_weight, 0)
    expand(0)
    expand(1)
    exchange(0, 1)
    exchange(*ISSUE[0])

    drain(wq.at[0, pl.ds(0, 256), :], w_r.at[1])
    remote(
        wq.at[0, pl.ds(0, 256), :], wq.at[0, pl.ds(256, 256), :], w_s.at[2], w_r.at[3], sibling
    ).start()
    drain(wbuf, a_r.at[WSTAGE])
    for_away(
        lambda to: remote(
            wrows(wbuf, to), wrows(wswap, to), ws_s.at[to], ws_r.at[to], z_peer
        ).start()
    )
    own_w.wait()
    drain(wq.at[1, pl.ds(256, 256), :], w_r.at[2])
    drain(wq.at[0, pl.ds(256, 256), :], w_r.at[3])

    def scale(h, d):
        wcol = wbuf[:, d : d + 1].astype(F32)
        for b in range(4):
            part = routed[h, d, :, b * 128 : b * 128 + 128].astype(F32) * wcol
            sct[h, b * 128 : b * 128 + 128, d * 256 : d * 256 + 256] = part.T.astype(BF16)

    def back_part(h, d, n):
        cols = pl.ds(pl.multiple_of(n * 256, 256), 256)
        return jnp.dot(routed[h, d], wq[h, :, cols], preferred_element_type=F32), cols

    def grad_down_part(h):
        def sib(n, carry):
            cols = pl.ds(pl.multiple_of(n * 256, 256), 256)
            csend[h, :, cols] = jnp.dot(
                sct[h, 256:512, :], act[:, cols], preferred_element_type=F32
            ).astype(BF16)
            return carry

        lax.fori_loop(0, 4, sib, 0)
        remote(csend.at[h], crecv.at[h], c_s.at[h], c_r.at[h], sibling).start()

        def own(n, carry):
            cols = pl.ds(pl.multiple_of(n * 256, 256), 256)
            pown[h, :, cols] = jnp.dot(sct[h, 0:256, :], act[:, cols], preferred_element_type=F32)
            return carry

        lax.fori_loop(0, 4, own, 0)

    def chip_sum():
        drain(crecv.at[0], c_r.at[0])

        def add(n, carry):
            rows = pl.ds(pl.multiple_of(n * 16, 16), 16)
            zsend[rows, :] = (pown[0, rows, :] + crecv[0, rows, :].astype(F32)).astype(BF16)
            return carry

        lax.fori_loop(0, 16, add, 0)

    def back_first(d):
        def one(n, carry):
            part, cols = back_part(0, d, n)
            bp[d, :, cols] = part
            return carry

        lax.fori_loop(0, 4, one, 0)

    def back_second(d):
        def one(n, carry):
            part, cols = back_part(1, d, n)
            if d:
                bsend[d - 1, :, cols] = (bp[d, :, cols] + part).astype(BF16)
            else:
                bp[0, :, cols] = bp[0, :, cols] + part
            return carry

        lax.fori_loop(0, 4, one, 0)
        if d:
            remote(
                bsend.at[d - 1], brecv.at[3 - d], b_s.at[d - 1], b_r.at[3 - d], at_x(d)
            ).start()

    def start_z(p):
        part = pl.ds(p * ZROWS, ZROWS)
        remote(zsend.at[part], zrecv.at[part], z_s.at[p], z_r.at[p], z_peer).start()

    arrived(0)
    exchange(*ISSUE[1])
    for d in (2, 1, 3):
        back_first(d)
    arrived(1)
    exchange(*ISSUE[2])
    back_second(2)
    arrived(2)
    back_second(1)
    arrived(3)
    back_second(3)
    for d in (1, 2, 3):
        drain(act.at[pl.ds(d * 256, 256)], act_r.at[d])
    for d in (2, 1, 3):
        scale(0, d)
    arrived(4)
    scale(0, 0)
    grad_down_part(0)
    for d in (2, 1, 3):
        scale(1, d)
    chip_sum()
    arrived(5)
    for p in range(ZFIRST):
        start_z(p)
    scale(1, 0)
    grad_down_part(1)
    back_first(0)
    back_second(0)

    for d in range(3):
        drain(brecv.at[d], b_r.at[d])

    def sum_rows(to):
        rows = pl.ds(pl.multiple_of(to * CAP, CAP), CAP)
        back = bp[0, rows, :] + brecv[0, rows, :].astype(F32)
        return rows, back + brecv[1, rows, :].astype(F32) + brecv[2, rows, :].astype(F32)

    def give(to):
        rows, back = sum_rows(to)
        bgive[rows, :] = back.astype(BF16)
        remote(wrows(bgive, to), wrows(btake, to), bs_s.at[to], bs_r.at[to], z_peer).start()

    for_away(give)
    for p in range(ZFIRST, ZPARTS):
        start_z(p)

    def finish(to, rows, back, weight):
        slot_grad = jnp.sum(acth[rows, :].astype(F32) * back, axis=1, keepdims=True)
        sgb[rows, :] = jnp.broadcast_to(slot_grad, (CAP, 128))
        bp[0, rows, :] = weight.astype(F32) * back

    def send_back(to):
        remote(wrows(sgb, to), wrows(ret, e), ret_s, ret_r, (f, to)).start()

    def finish_home(to, carry):
        @pl.when(away(to) == 0)
        def _():
            rows, back = sum_rows(to)
            finish(to, rows, back, wbuf[rows, 0:1])

            @pl.when(to != e)
            def _():
                send_back(to)

        return carry

    lax.fori_loop(0, ne, finish_home, 0)
    pltpu.make_async_copy(wrows(sgb, e), wrows(ret, e), ret_r).start()

    def grad_pre(rows):
        hidden = bp[0, rows, :]
        gp_out[rows, 0:1024] = (hidden * bvec[rows, 0:1024]).astype(BF16)
        gp_out[rows, 1024:2048] = (hidden * bvec[rows, 1024:2048]).astype(BF16)

    def grad_pre_home(to, carry):
        @pl.when(away(to) == 0)
        def _():
            grad_pre(pl.ds(pl.multiple_of(to * CAP, CAP), CAP))

        return carry

    lax.fori_loop(0, ne, grad_pre_home, 0)

    def finish_away(to):
        rows = pl.ds(pl.multiple_of(to * CAP, CAP), CAP)
        drain(wrows(btake, to), bs_r.at[to])
        drain(wrows(wswap, to), ws_r.at[to])
        finish(to, rows, btake[rows, :].astype(F32), wswap[rows, 0:1])
        send_back(to)

    for_away(finish_away)
    for_away(lambda to: grad_pre(pl.ds(pl.multiple_of(to * CAP, CAP), CAP)))

    drain(crecv.at[1], c_r.at[1])

    def chip_total(n, carry):
        rows = pl.ds(pl.multiple_of(n * 16, 16), 16)
        pown[1, rows, :] = pown[1, rows, :] + crecv[1, rows, :].astype(F32)
        return carry

    lax.fori_loop(0, 16, chip_total, 0)

    def total(n, carry):
        rows = pl.ds(pl.multiple_of(n * 16, 16), 16)
        gd_out[rows, :] = pown[1, rows, :] + zrecv[rows, :].astype(F32)
        return carry


    drain(ret, ret_r)
    per_slot = (gbuf[0].astype(F32) * ret[...]).reshape(ne, CAP, 128)
    per_expert = jnp.sum(per_slot, axis=1)
    ids8 = meta[0, 0:8, :]
    dp = jnp.zeros((8, 128), F32)
    for k in range(ne):
        dp = dp + jnp.where(ids8 == float(k), per_expert[k : k + 1, :], 0.0)
    dp_out[...] = dp

    for p in range(ZPARTS):
        drain(zrecv.at[pl.ds(p * ZROWS, ZROWS)], z_r.at[p])
        lax.fori_loop(p * ZROWS // 16, (p + 1) * ZROWS // 16, total, 0)

    def left(to):
        drain(wrows(acth, to), as_s.at[to])
        drain(wrows(wbuf, to), ws_s.at[to])
        drain(wrows(bgive, to), bs_s.at[to])

    for_away(left)
    for d in (1, 2, 3):
        drain(meta.at[0], meta_s.at[d])
        for h in range(2):
            drain(ogb.at[0, h], og_s.at[h, d])
        drain(act.at[pl.ds(0, 256)], act_s.at[d])
        drain(bsend.at[0], b_s.at[d - 1])
    for i in range(3):
        drain(wq.at[0, pl.ds(0, 256), :], w_s.at[i])
    for h in range(2):
        drain(csend.at[h], c_s.at[h])
    for p in range(ZPARTS):
        drain(zsend.at[pl.ds(p * ZROWS, ZROWS)], z_s.at[p])
    for i, (h, d0, dn) in enumerate(STAGES):
        drain(sendbuf.at[h, pl.ds(d0, dn), pl.ds(0, (ne - 1) * CAP), :], a_s.at[i])
    drain(wsend.at[pl.ds(0, (ne - 1) * CAP)], a_s.at[WSTAGE])
    drain(sgb.at[pl.ds(0, (ne - 1) * CAP)], ret_s)


def write_out(dp, gp, gd, dp_out, gp_out, gd_out, sem):
    copies = [
        pltpu.make_async_copy(src, dst, sem.at[i])
        for i, (src, dst) in enumerate(((gp, gp_out), (gd, gd_out), (dp, dp_out)))
    ]
    for copy in copies:
        copy.start()
    for copy in copies:
        copy.wait()


def per_device(out_grad, router_probs, expert_ids, saved_hidden, w_down):
    dma = pltpu.SemaphoreType.DMA
    vmem = pl.BlockSpec(memory_space=pltpu.VMEM)
    hbm = pl.BlockSpec(memory_space=pl.ANY)
    stages = len(STAGES) + 1
    dp, gp, gd = pl.pallas_call(
        kernel,
        out_shape=(
            pltpu.VMEM((8, 128), F32),
            pltpu.VMEM((256, 2048), BF16),
            pltpu.VMEM((256, 1024), F32),
        ),
        in_specs=[hbm] * 5,
        out_specs=(vmem, vmem, vmem),
        scratch_shapes=[
            pltpu.VMEM((4, 16, 128), F32),
            pltpu.VMEM((4, 2, 128, 512), BF16),
            pltpu.VMEM((4, 256, 128), BF16),
            pltpu.VMEM((256, 128), BF16),
            pltpu.VMEM((256, 128), BF16),
            pltpu.VMEM((2, 4, 256, 512), BF16),
            pltpu.VMEM((2, 4, 256, 512), BF16),
            pltpu.VMEM((256, 2048), BF16),
            pltpu.VMEM((1024, 1024), BF16),
            pltpu.VMEM((256, 2048), F32),
            pltpu.VMEM((2, 512, 1024), BF16),
            pltpu.VMEM((2, 512, 1024), BF16),
            pltpu.VMEM((2, 256, 1024), F32),
            pltpu.VMEM((2, 256, 1024), BF16),
            pltpu.VMEM((2, 256, 1024), BF16),
            pltpu.VMEM((256, 1024), BF16),
            pltpu.VMEM((256, 1024), BF16),
            pltpu.VMEM((4, 256, 1024), F32),
            pltpu.VMEM((3, 256, 1024), BF16),
            pltpu.VMEM((3, 256, 1024), BF16),
            pltpu.VMEM((256, 128), F32),
            pltpu.VMEM((256, 128), F32),
            pltpu.VMEM((8, 128), jnp.int32),
            pltpu.VMEM((8, 128), BF16),
            dma((2,)),
            dma,
            dma((4,)), dma((4,)),
            dma((2, 4)), dma((2, 4)),
            dma((3,)), dma((4,)),
            dma((4,)), dma((4,)),
            dma((stages,)), dma((stages,)),
            dma((2,)), dma((2,)),
            dma((ZPARTS,)), dma((ZPARTS,)),
            dma((3,)), dma((3,)),
            dma, dma,
            pltpu.VMEM((256, 1024), BF16),
            pltpu.VMEM((256, 128), BF16),
            pltpu.VMEM((256, 1024), BF16),
            pltpu.VMEM((256, 1024), BF16),
            dma((16,)), dma((16,)),
            dma((16,)), dma((16,)),
            dma((16,)), dma((16,)),
        ],
        compiler_params=pltpu.CompilerParams(
            collective_id=0, has_side_effects=True, vmem_limit_bytes=56 * 2**20
        ),
    )(
        expert_ids.T,
        router_probs.T,
        out_grad,
        saved_hidden.reshape(256, 2048),
        w_down.reshape(256, 1024),
    )
    dp, gp, gd = pl.pallas_call(
        write_out,
        out_shape=(
            jax.ShapeDtypeStruct((8, 128), F32),
            jax.ShapeDtypeStruct((256, 2048), BF16),
            jax.ShapeDtypeStruct((256, 1024), F32),
        ),
        in_specs=[hbm] * 3,
        out_specs=(hbm,) * 3,
        scratch_shapes=[dma((3,))],
    )(*(pltpu.with_memory_space_constraint(v, pltpu.VMEM) for v in (dp, gp, gd)))
    return dp.T, gp.reshape(1, 1, 256, 2048), gd.reshape(1, 256, 1024)


def solution(mesh):
    placed = (
        P(("fsdp", "expert"), None),
        P(("fsdp", "expert"), None),
        P(("fsdp", "expert"), None),
        P("fsdp", "expert", None, None),
        P("expert", "fsdp", None),
    )
    return jax.shard_map(
        per_device,
        mesh=mesh,
        in_specs=placed,
        out_specs=(
            P(("fsdp", "expert"), None),
            P("fsdp", "expert", None, None),
            P("expert", "fsdp", None),
        ),
        check_vma=False,
    )
```

```python
import jax
import jax.numpy as jnp
from jax import lax
from jax.experimental import pallas as pl
from jax.experimental.pallas import tpu as pltpu
from jax.sharding import PartitionSpec as P

F32 = jnp.float32
BF16 = jnp.bfloat16
MESH = pl.DeviceIdType.MESH
CAP = 16
NX = 4
STAGES = ((0, 1, 3), (1, 2, 1), (1, 1, 1), (1, 3, 1), (0, 0, 1), (1, 0, 1))
WSTAGE = len(STAGES)
ISSUE = ((1, 5), (6, 0), (6, 0))
ZROWS = ((0, 160), (160, 96))
ZPARTS = 2
ZFIRST = 1


def kernel(
    ids_hbm, probs_hbm, og_hbm, hid_hbm, w_hbm,
    dp_out, gp_out, gd_out,
    meta, ogb, gbuf, wsend, wbuf, sendbuf, routed, hidv, act, bvec, wq, sct, pown,
    csend, crecv, zsend, zrecv, bp, bsend, brecv, sgb, ret,
    ids_ref, probs_ref, in_sem, hid_sem, meta_s, meta_r, og_s, og_r, w_s, w_r, act_s, act_r, a_s, a_r,
    c_s, c_r, z_s, z_r, b_s, b_r, ret_s, ret_r,
    acth, wswap, bgive, btake, as_s, as_r, ws_s, ws_r, bs_s, bs_r,
):
    ne = 16
    f = lax.axis_index("fsdp")
    e = lax.axis_index("expert")
    zh, x, c = f // 8, (f // 2) % 4, f % 2
    zl, y = e // 4, e % 4

    def at_x(d):
        return (zh * 8 + ((x + d) % 4) * 2 + c, e)

    z_peer = ((1 - zh) * 8 + x * 2 + c, e)
    sibling = (zh * 8 + x * 2 + 1 - c, e)

    def away(to):
        gap = (zl - to // 4) * (zl - to // 4)
        return gap // 9 + ((gap // 4) % 2) * ((y + to % 4) % 2)

    def near(to):
        return (((zh + away(to)) % 2) * 8 + x * 2 + c, to)

    def for_away(do):
        def one(to, carry):
            @pl.when(away(to) == 1)
            def _():
                do(to)

            return carry

        lax.fori_loop(0, ne, one, 0)

    def remote(src, dst, ss, rs, dev):
        return pltpu.make_async_remote_copy(
            src_ref=src, dst_ref=dst, send_sem=ss, recv_sem=rs, device_id=dev, device_id_type=MESH
        )

    def drain(ref, sem):
        pltpu.make_async_copy(ref, ref, sem).wait()

    own_w = pltpu.make_async_copy(w_hbm, wq.at[1, pl.ds(0, 256), :], w_r.at[0])
    own_hid = pltpu.make_async_copy(hid_hbm, hidv, hid_sem)

    def og_columns(xt, h):
        col = ((zh + 1 - h) % 2) * 2048 + xt * 512
        return og_hbm.at[:, pl.ds(pl.multiple_of(col, 512), 512)]

    barrier = pltpu.get_barrier_semaphore()
    for d in (1, 2, 3):
        pl.semaphore_signal(barrier, inc=1, device_id=at_x(d), device_id_type=MESH)
    pl.semaphore_signal(barrier, inc=1, device_id=z_peer, device_id_type=MESH)
    pl.semaphore_signal(barrier, inc=1, device_id=sibling, device_id_type=MESH)

    def greet(k, carry):
        to = (e + k) % ne
        pl.semaphore_signal(barrier, inc=1, device_id=near(to), device_id_type=MESH)

        @pl.when(away(to) == 1)
        def _():
            pl.semaphore_signal(barrier, inc=1, device_id=(f, to), device_id_type=MESH)

        return carry + away(to)

    extra = lax.fori_loop(1, ne, greet, 0)
    for h in range(2):
        pltpu.make_async_copy(og_columns(x, h), ogb.at[0, h], og_r.at[h, 0]).start()
    own_hid.start()
    own_w.start()
    own_ids = pltpu.make_async_copy(ids_hbm, ids_ref, in_sem.at[0])
    own_probs = pltpu.make_async_copy(probs_hbm, probs_ref, in_sem.at[1])
    own_ids.start()
    own_probs.start()
    own_ids.wait()
    own_probs.wait()
    meta[0, 0:8, :] = ids_ref[...].astype(F32)
    meta[0, 8:16, :] = probs_ref[...].astype(F32)

    own_hid.wait()

    def wrows(ref, who):
        return ref.at[pl.ds(pl.multiple_of(who * CAP, CAP), CAP), :]

    def activate(i, carry):
        rows = pl.ds(pl.multiple_of(i * CAP, CAP), CAP)
        gate = hidv[rows, 0:1024].astype(F32)
        up = hidv[rows, 1024:2048].astype(F32)
        sigma = jax.nn.sigmoid(gate)
        silu = gate * sigma
        bvec[rows, 0:1024] = up * sigma * (1.0 + gate * (1.0 - sigma))
        bvec[rows, 1024:2048] = silu
        value = (silu * up).astype(BF16)
        acth[rows, :] = value

        @pl.when(away(i) == 0)
        def _():
            act[rows, :] = value

        return carry

    lax.fori_loop(0, ne, activate, 0)
    pl.semaphore_wait(barrier, 5 + ne - 1 + extra)
    for_away(
        lambda to: remote(
            wrows(acth, to), wrows(act, to), as_s.at[to], as_r.at[to], z_peer
        ).start()
    )

    for d in (2, 1, 3):
        remote(meta.at[0], meta.at[4 - d], meta_s.at[d], meta_r.at[4 - d], at_x(d)).start()
    for h in range(2):
        for d in (2, 1, 3):
            remote(
                og_columns((x + d) % 4, h),
                ogb.at[4 - d, h],
                og_s.at[h, d],
                og_r.at[h, 4 - d],
                at_x(d),
            ).start()
        if h == 0:
            remote(w_hbm, wq.at[0, pl.ds(0, 256), :], w_s.at[0], w_r.at[1], z_peer).start()
            remote(w_hbm, wq.at[1, pl.ds(256, 256), :], w_s.at[1], w_r.at[2], sibling).start()

    tri_r = lax.broadcasted_iota(jnp.int32, (128, 128), 0)
    tri_c = lax.broadcasted_iota(jnp.int32, (128, 128), 1)
    upper = jnp.where(tri_r < tri_c, 1.0, 0.0).astype(BF16)
    e_iota = lax.broadcasted_iota(jnp.int32, (ne, 128), 0).astype(F32)
    r_iota = lax.broadcasted_iota(jnp.int32, (ne, CAP, 128), 1).astype(F32)
    lane = lax.broadcasted_iota(jnp.int32, (ne * CAP, 128), 1)
    wacc = jnp.zeros((ne * CAP, 128), F32)
    for d in (0, 1, 3, 2):
        if d:
            drain(meta.at[d], meta_r.at[d])
        ids8 = meta[d, 0:8, :]
        pr8 = meta[d, 8:16, :]
        named = jnp.zeros((ne, 128), F32)
        prob = jnp.zeros((ne, 128), F32)
        for k in range(8):
            hit = ids8[k : k + 1, :] == e_iota
            named = named + jnp.where(hit, 1.0, 0.0)
            prob = prob + jnp.where(hit, pr8[k : k + 1, :], 0.0)
        rank = jnp.dot(named.astype(BF16), upper, preferred_element_type=F32)
        rank = jnp.where(named > 0.0, rank, -1.0)
        pick = jnp.where(rank[:, None, :] == r_iota, 1.0, 0.0)
        wcol = jnp.sum((pick * prob[:, None, :]).reshape(ne * CAP, 128), axis=1, keepdims=True)
        wacc = jnp.where(lane == d, wcol, wacc)
        gbuf[d] = pick.reshape(ne * CAP, 128).astype(BF16)
    wsend[...] = wacc.astype(BF16)

    for_away(lambda to: drain(wrows(act, to), as_r.at[to]))
    for d in (2, 1, 3):
        remote(
            act.at[pl.ds(0, 256)],
            act.at[pl.ds((4 - d) * 256, 256)],
            act_s.at[d],
            act_r.at[4 - d],
            at_x(d),
        ).start()

    def expand(h):
        for d in (0, 1, 3, 2):
            drain(ogb.at[d, h], og_r.at[h, d])
            for dc in range(2):
                columns = pl.ds(pl.multiple_of(((c + dc) % 2) * 256, 256), 256)
                sendbuf[h, d, :, dc * 256 : dc * 256 + 256] = jnp.dot(
                    gbuf[d], ogb[d, h, :, columns], preferred_element_type=F32
                ).astype(BF16)

    def my_rows(ref, h, d0, dn, who):
        return ref.at[h, pl.ds(d0, dn), pl.ds(pl.multiple_of(who * CAP, CAP), CAP), :]

    def exchange(first, count):
        for i in range(first, first + count):
            h, d0, dn = STAGES[i]
            pltpu.make_async_copy(
                my_rows(sendbuf, h, d0, dn, e), my_rows(routed, h, d0, dn, e), a_r.at[i]
            ).start()

            def send(k, carry):
                to = (e + k) % ne
                remote(
                    my_rows(sendbuf, (h + away(to)) % 2, d0, dn, to),
                    my_rows(routed, h, d0, dn, e),
                    a_s.at[i],
                    a_r.at[i],
                    near(to),
                ).start()
                return carry

            lax.fori_loop(1, ne, send, 0)

    def arrived(i):
        h, d0, dn = STAGES[i]
        drain(routed.at[h, pl.ds(d0, dn)], a_r.at[i])

    pltpu.make_async_copy(wrows(wsend, e), wrows(wbuf, e), a_r.at[WSTAGE]).start()

    def send_weight(k, carry):
        to = (e + k) % ne
        remote(
            wrows(wsend, to), wrows(wbuf, e), a_s.at[WSTAGE], a_r.at[WSTAGE], near(to)
        ).start()
        return carry

    lax.fori_loop(1, ne, send_weight, 0)
    expand(0)
    expand(1)
    exchange(0, 1)
    exchange(*ISSUE[0])

    drain(wq.at[0, pl.ds(0, 256), :], w_r.at[1])
    remote(
        wq.at[0, pl.ds(0, 256), :], wq.at[0, pl.ds(256, 256), :], w_s.at[2], w_r.at[3], sibling
    ).start()
    drain(wbuf, a_r.at[WSTAGE])
    for_away(
        lambda to: remote(
            wrows(wbuf, to), wrows(wswap, to), ws_s.at[to], ws_r.at[to], z_peer
        ).start()
    )
    own_w.wait()
    drain(wq.at[1, pl.ds(256, 256), :], w_r.at[2])
    drain(wq.at[0, pl.ds(256, 256), :], w_r.at[3])

    def scale(h, d):
        wcol = wbuf[:, d : d + 1].astype(F32)
        for b in range(4):
            part = routed[h, d, :, b * 128 : b * 128 + 128].astype(F32) * wcol
            sct[h, b * 128 : b * 128 + 128, d * 256 : d * 256 + 256] = part.T.astype(BF16)

    def back_part(h, d, n):
        cols = pl.ds(pl.multiple_of(n * 256, 256), 256)
        return jnp.dot(routed[h, d], wq[h, :, cols], preferred_element_type=F32), cols

    def grad_down_part(h):
        def sib(n, carry):
            cols = pl.ds(pl.multiple_of(n * 256, 256), 256)
            csend[h, :, cols] = jnp.dot(
                sct[h, 256:512, :], act[:, cols], preferred_element_type=F32
            ).astype(BF16)
            return carry

        lax.fori_loop(0, 4, sib, 0)
        remote(csend.at[h], crecv.at[h], c_s.at[h], c_r.at[h], sibling).start()

        def own(n, carry):
            cols = pl.ds(pl.multiple_of(n * 256, 256), 256)
            pown[h, :, cols] = jnp.dot(sct[h, 0:256, :], act[:, cols], preferred_element_type=F32)
            return carry

        lax.fori_loop(0, 4, own, 0)

    def chip_sum():
        drain(crecv.at[0], c_r.at[0])

        def add(n, carry):
            rows = pl.ds(pl.multiple_of(n * 16, 16), 16)
            zsend[rows, :] = (pown[0, rows, :] + crecv[0, rows, :].astype(F32)).astype(BF16)
            return carry

        lax.fori_loop(0, 16, add, 0)

    def back_first(d):
        def one(n, carry):
            part, cols = back_part(0, d, n)
            bp[d, :, cols] = part
            return carry

        lax.fori_loop(0, 4, one, 0)

    def back_second(d):
        def one(n, carry):
            part, cols = back_part(1, d, n)
            if d:
                bsend[d - 1, :, cols] = (bp[d, :, cols] + part).astype(BF16)
            else:
                bp[0, :, cols] = bp[0, :, cols] + part
            return carry

        lax.fori_loop(0, 4, one, 0)
        if d:
            remote(
                bsend.at[d - 1], brecv.at[3 - d], b_s.at[d - 1], b_r.at[3 - d], at_x(d)
            ).start()

    def start_z(p):
        part = pl.ds(*ZROWS[p])
        remote(zsend.at[part], zrecv.at[part], z_s.at[p], z_r.at[p], z_peer).start()

    arrived(0)
    exchange(*ISSUE[1])
    for d in (2, 1, 3):
        back_first(d)
    arrived(1)
    exchange(*ISSUE[2])
    back_second(2)
    arrived(2)
    back_second(1)
    arrived(3)
    back_second(3)
    for d in (1, 2, 3):
        drain(act.at[pl.ds(d * 256, 256)], act_r.at[d])
    for d in (2, 1, 3):
        scale(0, d)
    arrived(4)
    scale(0, 0)
    grad_down_part(0)
    for d in (2, 1, 3):
        scale(1, d)
    chip_sum()
    arrived(5)
    for p in range(ZFIRST):
        start_z(p)
    scale(1, 0)
    grad_down_part(1)
    back_first(0)
    back_second(0)

    for d in range(3):
        drain(brecv.at[d], b_r.at[d])

    def sum_rows(to):
        rows = pl.ds(pl.multiple_of(to * CAP, CAP), CAP)
        back = bp[0, rows, :] + brecv[0, rows, :].astype(F32)
        return rows, back + brecv[1, rows, :].astype(F32) + brecv[2, rows, :].astype(F32)

    def give(to):
        rows, back = sum_rows(to)
        bgive[rows, :] = back.astype(BF16)
        remote(wrows(bgive, to), wrows(btake, to), bs_s.at[to], bs_r.at[to], z_peer).start()

    for_away(give)
    for p in range(ZFIRST, ZPARTS):
        start_z(p)

    def finish(to, rows, back, weight):
        slot_grad = jnp.sum(acth[rows, :].astype(F32) * back, axis=1, keepdims=True)
        sgb[rows, :] = jnp.broadcast_to(slot_grad, (CAP, 128))
        bp[0, rows, :] = weight.astype(F32) * back

    def send_back(to):
        remote(wrows(sgb, to), wrows(ret, e), ret_s, ret_r, (f, to)).start()

    def finish_home(to, carry):
        @pl.when(away(to) == 0)
        def _():
            rows, back = sum_rows(to)
            finish(to, rows, back, wbuf[rows, 0:1])

            @pl.when(to != e)
            def _():
                send_back(to)

        return carry

    lax.fori_loop(0, ne, finish_home, 0)
    pltpu.make_async_copy(wrows(sgb, e), wrows(ret, e), ret_r).start()

    def grad_pre(rows):
        hidden = bp[0, rows, :]
        gp_out[rows, 0:1024] = (hidden * bvec[rows, 0:1024]).astype(BF16)
        gp_out[rows, 1024:2048] = (hidden * bvec[rows, 1024:2048]).astype(BF16)

    def grad_pre_home(to, carry):
        @pl.when(away(to) == 0)
        def _():
            grad_pre(pl.ds(pl.multiple_of(to * CAP, CAP), CAP))

        return carry

    lax.fori_loop(0, ne, grad_pre_home, 0)

    def finish_away(to):
        rows = pl.ds(pl.multiple_of(to * CAP, CAP), CAP)
        drain(wrows(btake, to), bs_r.at[to])
        drain(wrows(wswap, to), ws_r.at[to])
        finish(to, rows, btake[rows, :].astype(F32), wswap[rows, 0:1])
        send_back(to)

    for_away(finish_away)
    for_away(lambda to: grad_pre(pl.ds(pl.multiple_of(to * CAP, CAP), CAP)))

    drain(crecv.at[1], c_r.at[1])

    def chip_total(n, carry):
        rows = pl.ds(pl.multiple_of(n * 16, 16), 16)
        pown[1, rows, :] = pown[1, rows, :] + crecv[1, rows, :].astype(F32)
        return carry

    lax.fori_loop(0, 16, chip_total, 0)

    def total(n, carry):
        rows = pl.ds(pl.multiple_of(n * 16, 16), 16)
        gd_out[rows, :] = pown[1, rows, :] + zrecv[rows, :].astype(F32)
        return carry


    drain(ret, ret_r)
    per_slot = (gbuf[0].astype(F32) * ret[...]).reshape(ne, CAP, 128)
    per_expert = jnp.sum(per_slot, axis=1)
    ids8 = meta[0, 0:8, :]
    dp = jnp.zeros((8, 128), F32)
    for k in range(ne):
        dp = dp + jnp.where(ids8 == float(k), per_expert[k : k + 1, :], 0.0)
    dp_out[...] = dp

    for p in range(ZPARTS):
        drain(zrecv.at[pl.ds(*ZROWS[p])], z_r.at[p])
        lax.fori_loop(ZROWS[p][0] // 16, sum(ZROWS[p]) // 16, total, 0)

    def left(to):
        drain(wrows(acth, to), as_s.at[to])
        drain(wrows(wbuf, to), ws_s.at[to])
        drain(wrows(bgive, to), bs_s.at[to])

    for_away(left)
    for d in (1, 2, 3):
        drain(meta.at[0], meta_s.at[d])
        for h in range(2):
            drain(ogb.at[0, h], og_s.at[h, d])
        drain(act.at[pl.ds(0, 256)], act_s.at[d])
        drain(bsend.at[0], b_s.at[d - 1])
    for i in range(3):
        drain(wq.at[0, pl.ds(0, 256), :], w_s.at[i])
    for h in range(2):
        drain(csend.at[h], c_s.at[h])
    for p in range(ZPARTS):
        drain(zsend.at[pl.ds(*ZROWS[p])], z_s.at[p])
    for i, (h, d0, dn) in enumerate(STAGES):
        drain(sendbuf.at[h, pl.ds(d0, dn), pl.ds(0, (ne - 1) * CAP), :], a_s.at[i])
    drain(wsend.at[pl.ds(0, (ne - 1) * CAP)], a_s.at[WSTAGE])
    drain(sgb.at[pl.ds(0, (ne - 1) * CAP)], ret_s)


def write_out(dp, gp, gd, dp_out, gp_out, gd_out, sem):
    copies = [
        pltpu.make_async_copy(src, dst, sem.at[i])
        for i, (src, dst) in enumerate(((gp, gp_out), (gd, gd_out), (dp, dp_out)))
    ]
    for copy in copies:
        copy.start()
    for copy in copies:
        copy.wait()


def per_device(out_grad, router_probs, expert_ids, saved_hidden, w_down):
    dma = pltpu.SemaphoreType.DMA
    vmem = pl.BlockSpec(memory_space=pltpu.VMEM)
    hbm = pl.BlockSpec(memory_space=pl.ANY)
    stages = len(STAGES) + 1
    dp, gp, gd = pl.pallas_call(
        kernel,
        out_shape=(
            pltpu.VMEM((8, 128), F32),
            pltpu.VMEM((256, 2048), BF16),
            pltpu.VMEM((256, 1024), F32),
        ),
        in_specs=[hbm] * 5,
        out_specs=(vmem, vmem, vmem),
        scratch_shapes=[
            pltpu.VMEM((4, 16, 128), F32),
            pltpu.VMEM((4, 2, 128, 512), BF16),
            pltpu.VMEM((4, 256, 128), BF16),
            pltpu.VMEM((256, 128), BF16),
            pltpu.VMEM((256, 128), BF16),
            pltpu.VMEM((2, 4, 256, 512), BF16),
            pltpu.VMEM((2, 4, 256, 512), BF16),
            pltpu.VMEM((256, 2048), BF16),
            pltpu.VMEM((1024, 1024), BF16),
            pltpu.VMEM((256, 2048), F32),
            pltpu.VMEM((2, 512, 1024), BF16),
            pltpu.VMEM((2, 512, 1024), BF16),
            pltpu.VMEM((2, 256, 1024), F32),
            pltpu.VMEM((2, 256, 1024), BF16),
            pltpu.VMEM((2, 256, 1024), BF16),
            pltpu.VMEM((256, 1024), BF16),
            pltpu.VMEM((256, 1024), BF16),
            pltpu.VMEM((4, 256, 1024), F32),
            pltpu.VMEM((3, 256, 1024), BF16),
            pltpu.VMEM((3, 256, 1024), BF16),
            pltpu.VMEM((256, 128), F32),
            pltpu.VMEM((256, 128), F32),
            pltpu.VMEM((8, 128), jnp.int32),
            pltpu.VMEM((8, 128), BF16),
            dma((2,)),
            dma,
            dma((4,)), dma((4,)),
            dma((2, 4)), dma((2, 4)),
            dma((3,)), dma((4,)),
            dma((4,)), dma((4,)),
            dma((stages,)), dma((stages,)),
            dma((2,)), dma((2,)),
            dma((ZPARTS,)), dma((ZPARTS,)),
            dma((3,)), dma((3,)),
            dma, dma,
            pltpu.VMEM((256, 1024), BF16),
            pltpu.VMEM((256, 128), BF16),
            pltpu.VMEM((256, 1024), BF16),
            pltpu.VMEM((256, 1024), BF16),
            dma((16,)), dma((16,)),
            dma((16,)), dma((16,)),
            dma((16,)), dma((16,)),
        ],
        compiler_params=pltpu.CompilerParams(
            collective_id=0, has_side_effects=True, vmem_limit_bytes=56 * 2**20
        ),
    )(
        expert_ids.T,
        router_probs.T,
        out_grad,
        saved_hidden.reshape(256, 2048),
        w_down.reshape(256, 1024),
    )
    dp, gp, gd = pl.pallas_call(
        write_out,
        out_shape=(
            jax.ShapeDtypeStruct((8, 128), F32),
            jax.ShapeDtypeStruct((256, 2048), BF16),
            jax.ShapeDtypeStruct((256, 1024), F32),
        ),
        in_specs=[hbm] * 3,
        out_specs=(hbm,) * 3,
        scratch_shapes=[dma((3,))],
    )(*(pltpu.with_memory_space_constraint(v, pltpu.VMEM) for v in (dp, gp, gd)))
    return dp.T, gp.reshape(1, 1, 256, 2048), gd.reshape(1, 256, 1024)


def solution(mesh):
    placed = (
        P(("fsdp", "expert"), None),
        P(("fsdp", "expert"), None),
        P(("fsdp", "expert"), None),
        P("fsdp", "expert", None, None),
        P("expert", "fsdp", None),
    )
    return jax.shard_map(
        per_device,
        mesh=mesh,
        in_specs=placed,
        out_specs=(
            P(("fsdp", "expert"), None),
            P("fsdp", "expert", None, None),
            P("expert", "fsdp", None),
        ),
        check_vma=False,
    )
```
